128 devices in a mesh: grp: 4 (over y), dev: 32 (over x, z, core).
Axes of the slice: x: 4, y: 4, z: 4, core: 2. Of those that a mesh axis runs over, the one named last changes fastest.
Arguments:
- captions: bfloat16 [32, 64, 4096], P('dev', 'grp'), may hold values from -6 to 6
- kv_weight: bfloat16 [4096, 2048], P('grp'), may hold values from -0.09375 to 0.09375
- image_tokens: bfloat16 [512, 256, 2048], P(('grp', 'dev')), may hold values from -28 to 28
- q_weight: bfloat16 [2048, 1024], replicated, may hold values from -0.125 to 0.125
- context_grad: bfloat16 [512, 256, 1024], P(('grp', 'dev')), may hold values from -6 to 6
- sample_prompt: int32 [512], replicated, may hold values from 0 to 31
- caption_len: int32 [32], replicated, may hold values from 8 to 64
Outputs:
- context: bfloat16 [512, 256, 1024], P(('grp', 'dev'))
- image_grad: bfloat16 [512, 256, 2048], P(('grp', 'dev'))
- caption_grad: float32 [32, 64, 4096], P('dev', 'grp')
The draws below stay inside these ranges and needn't reach their ends.
Inputs may be any that keep to these rules, and one draw needn't show every extreme that they name: `sample_prompt`: sample s belongs to the device at position s // 4 of the devices taken with grp slowest; a prompt may have no samples.
All inputs are finite; a program needn't handle non-finite values.
Results may differ from the reference program's by a relative error of at most 0.008.
Values may be sent and summed in bfloat16 or wider, within the bound.
A program may use at most 128 MiB of HBM per device.

```python
import math
import jax
import jax.numpy as jnp
import numpy as np
from jax import lax

E = 4096
C = 2048
HEADS = 8
HD = 128
INNER = 1024
L = 64
IMG = 256
PROMPTS = 32
SAMPLES = 512


def draw_image_tokens(key, part):
    first_key = jax.random.fold_in(jax.random.fold_in(key, 17), 0)
    return jnp.clip(jax.random.normal(first_key, (SAMPLES, IMG, C), jnp.float32), -6.0, 6.0).astype(jnp.bfloat16)


def plant(drawn, rng, least, high):
    extent = drawn.shape
    spot = [jax.random.randint(jax.random.fold_in(rng, axis), (), 0, extent[axis]) for axis in range(len(extent))]
    drawn = drawn.at[tuple(spot)].set(least)
    longest = extent.index(max(extent))
    spot[longest] = (spot[longest] + 1) % extent[longest]
    return drawn.at[tuple(spot)].set(high)


def levels(own_key, extent, cuts, smallest, largest):
    def one(position, shards_of):
        steps = jax.random.uniform(jax.random.fold_in(jax.random.fold_in(own_key, 6), position), (shards_of,), jnp.float32, smallest / len(cuts), largest / len(cuts))
        return jnp.repeat(jnp.exp(steps), extent[position] // shards_of).reshape((-1,) + (1,) * (len(extent) - position - 1))

    loudness = one(*cuts[0])
    for cut in cuts[1:]:
        loudness = loudness * one(*cut)
    return loudness


def rank_bounds(count, skew):
    portions = [(1 << 20) // math.isqrt(rank ** skew) + 1 for rank in range(1, count + 1)]
    deviation = 1 + sum(portions) // (1 << 30)
    return np.cumsum(np.array([max(1, weight // deviation) for weight in portions]))


def ranked(rng, shape, amount, slope):
    listing = rank_bounds(amount, slope)
    pick = jax.random.randint(jax.random.fold_in(rng, 1), shape, 0, int(listing[amount - 1]))
    grade = jnp.searchsorted(jnp.asarray(listing, jnp.int32), pick, side="right")
    return jax.random.permutation(jax.random.fold_in(rng, 2), amount)[grade].astype(jnp.int32)


def scatter_about(stream_key, extent, spread, limit, cuts=(), held_as=jnp.bfloat16):
    level = levels(stream_key, extent, cuts, -0.22, 0.18) if cuts else 1.0
    entries = jax.random.normal(stream_key, extent, jnp.float32) * spread * level
    return jnp.minimum(jnp.maximum(entries, -limit), limit).astype(held_as)


def setup_inputs(seed: int = 0) -> dict:
    streams_of = jax.random.split(jax.random.key(seed), 8)
    return {
        "captions": scatter_about(streams_of[0], (PROMPTS, L, E), 1.0, 6.0, ((0, 32), (1, 4))),
        "kv_weight": scatter_about(streams_of[1], (E, 2 * INNER), E ** -0.5, 0.09375, ((0, 4),)),
        "image_tokens": draw_image_tokens(jax.random.fold_in(streams_of[7], 71), 0),
        "q_weight": scatter_about(streams_of[3], (C, INNER), C ** -0.5, 0.125),
        "context_grad": scatter_about(streams_of[4], (SAMPLES, IMG, INNER), 1.0, 6.0, ((0, 128),)),
        "sample_prompt": plant(ranked(streams_of[5], (SAMPLES,), PROMPTS, 2), jax.random.fold_in(streams_of[5], 3), 0, PROMPTS - 1).astype(jnp.int32),
        "caption_len": plant(jax.random.randint(streams_of[6], (PROMPTS,), L // 8, L + 1), jax.random.fold_in(streams_of[6], 1), L // 8, L).astype(jnp.int32),
    }


NEG_FILL = -1e+30

def attend_one(queries, key_rows, value_rows, live, grad_rows):
    score_scale = 1.0 / math.sqrt(HD)
    scores = jnp.einsum('ihd,jhd->hij', queries.astype(jnp.float32), key_rows.astype(jnp.float32)) * score_scale
    scores = jnp.where(live[None, None, :], scores, NEG_FILL)
    top_score = lax.optimization_barrier(jnp.max(scores, axis=-1, keepdims=True))
    expd = jnp.exp(scores - top_score)
    soft = expd / lax.optimization_barrier(jnp.sum(expd, axis=-1, keepdims=True))
    soft_b = soft.astype(jnp.bfloat16)
    context = jnp.einsum('hij,jhd->ihd', soft_b.astype(jnp.float32), value_rows.astype(jnp.float32)).astype(jnp.bfloat16)
    d_soft = jnp.einsum('ihd,jhd->hij', grad_rows.astype(jnp.float32), value_rows.astype(jnp.float32))
    d_values = jnp.einsum('hij,ihd->jhd', soft_b.astype(jnp.float32), grad_rows.astype(jnp.float32))
    d_scores = (soft * (d_soft - lax.optimization_barrier(jnp.sum(d_soft * soft, axis=-1, keepdims=True))) * score_scale).astype(jnp.bfloat16)
    d_keys = jnp.einsum('hij,ihd->jhd', d_scores.astype(jnp.float32), queries.astype(jnp.float32))
    d_queries = jnp.einsum('hij,jhd->ihd', d_scores.astype(jnp.float32), key_rows.astype(jnp.float32)).astype(jnp.bfloat16)
    return (context, d_queries, d_keys, d_values)

def reference(captions, kv_weight, image_tokens, q_weight, context_grad, sample_prompt, caption_len):
    kv_all = jnp.dot(captions.reshape(PROMPTS * L, E), kv_weight, preferred_element_type=jnp.float32)
    kv_all = kv_all.astype(jnp.bfloat16).reshape(PROMPTS, L, 2 * INNER)
    positions = jnp.arange(L, dtype=jnp.int32)

    def one_sample(carry, inputs):
        tokens_one, grad_one, prompt_id = inputs
        prompt_id = prompt_id.astype(jnp.int32)
        kv_rows = lax.dynamic_index_in_dim(kv_all, prompt_id, 0, keepdims=False)
        length = lax.dynamic_index_in_dim(caption_len, prompt_id, 0, keepdims=False)
        queries = jnp.dot(tokens_one, q_weight, preferred_element_type=jnp.float32).astype(jnp.bfloat16)
        queries = queries.reshape(IMG, HEADS, HD)
        key_rows = kv_rows[:, :INNER].reshape(L, HEADS, HD)
        value_rows = kv_rows[:, INNER:].reshape(L, HEADS, HD)
        live = positions < length
        context, d_queries, d_keys, d_values = attend_one(queries, key_rows, value_rows, live, grad_one.reshape(IMG, HEADS, HD))
        image_grad = jnp.dot(d_queries.reshape(IMG, INNER), q_weight.T, preferred_element_type=jnp.float32).astype(jnp.bfloat16)
        grad_kv = jnp.concatenate([d_keys.reshape(L, INNER), d_values.reshape(L, INNER)], axis=1)
        current = lax.dynamic_index_in_dim(carry, prompt_id, 0, keepdims=False)
        carry = lax.dynamic_update_index_in_dim(carry, current + grad_kv, prompt_id, 0)
        return (carry, (context.reshape(IMG, INNER), image_grad))
    start_sums = jnp.zeros((PROMPTS, L, 2 * INNER), jnp.float32)
    kv_grad, (context, image_grad) = lax.scan(one_sample, start_sums, (image_tokens, context_grad, sample_prompt))
    kv_grad_b = kv_grad.astype(jnp.bfloat16).reshape(PROMPTS * L, 2 * INNER)
    caption_grad = jnp.dot(kv_grad_b, kv_weight.T, preferred_element_type=jnp.float32).reshape(PROMPTS, L, E)
    return (context, image_grad, caption_grad)
```

```python
import functools
import math

import jax
import jax.numpy as jnp
from jax import lax
from jax.experimental import pallas as pl
from jax.experimental.pallas import tpu as pltpu
from jax.sharding import PartitionSpec as P

HEADS = 8
HD = 128
NEG_FILL = -1e30
MESH = pl.DeviceIdType.MESH
BF16 = jnp.bfloat16
F32 = jnp.float32
VMEM_LIMIT = 56 * 1024 * 1024

NY, NX, NZ, NC = 4, 4, 4, 2
SAMP = 4
TOK = 16
INNER = 1024
WIDE = 4096
DEPTH = 1024
IMG = 256
CIMG = 2048
PROMPTS = 32


def place():
    grp = lax.axis_index("grp")
    dev = lax.axis_index("dev")
    return grp, lax.div(dev, 8), lax.rem(lax.div(dev, 2), 4), lax.rem(dev, 2)


def at(grp, x, z, core):
    return {"grp": grp, "dev": (x * NZ + z) * NC + core}


def turn(index, step, size):
    return lax.rem(index + step, size)


def greet():
    y, x, z, c = place()
    barrier = pltpu.get_barrier_semaphore()
    peers = [at(turn(y, k, NY), x, z, turn(c, j, NC)) for k in range(NY) for j in range(NC) if k or j]
    peers += [at(y, turn(x, k, NX), z, c) for k in range(1, NX)]
    peers += [at(y, x, turn(z, k, NZ), c) for k in range(1, NZ)]
    for peer in peers:
        pl.semaphore_signal(barrier, inc=1, device_id=peer, device_id_type=MESH)
    pl.semaphore_wait(barrier, len(peers))


def send(src, dst, send_sem, recv_sem, peer):
    copy = pltpu.make_async_remote_copy(
        src_ref=src, dst_ref=dst, send_sem=send_sem, recv_sem=recv_sem, device_id=peer, device_id_type=MESH
    )
    copy.start()
    return copy


def front_kernel(
    prompt_ref, cap_ref, w_hbm, x_hbm, qw_hbm, q_out, kv_out,
    w_v, x_v, qw_v, q_v, caps, part, rs, kvb, gath, sel,
    load_sem, cap_s, cap_r, rs_s, rs_r, pair_s, pair_r, ag_s, ag_r, sel_s, sel_r, own_sem, q_sem,
):
    y, x, z, c = place()
    loads = [
        pltpu.make_async_copy(w_hbm, w_v, load_sem.at[0]),
        pltpu.make_async_copy(x_hbm, x_v, load_sem.at[1]),
        pltpu.make_async_copy(qw_hbm, qw_v, load_sem.at[2]),
    ]
    for load in loads:
        load.start()
    greet()

    def columns(index):
        return pl.ds(pl.multiple_of(index * DEPTH, DEPTH), DEPTH)

    sends = []
    for k in range(1, NY):
        to = turn(y, k, NY)
        sends.append(send(cap_ref.at[:, columns(to)], caps.at[y], cap_s.at[k], cap_r.at[k], at(to, x, z, c)))
    caps[pl.ds(y, 1)] = cap_ref[:, columns(y)][None]
    loads[0].wait()
    for copy in sends:
        copy.wait()

    lhs = caps[...].reshape(NY * TOK, DEPTH)
    sends = []
    step = 512
    for n in range(2 * INNER // step):
        cols = pl.ds(n * step, step)
        part[:, :, cols] = jnp.dot(lhs, w_v[:, cols], preferred_element_type=F32).reshape(NY, TOK, step)
        for k in range(1, NY):
            to = turn(y, k, NY)
            sends.append(
                send(part.at[to, :, cols], rs.at[k - 1, :, cols], rs_s.at[k, n], rs_r.at[k, n], at(to, x, z, c))
            )

    loads[1].wait()
    loads[2].wait()

    def project(tile):
        rows = pl.ds(tile * IMG, IMG)
        q_v[rows, :] = jnp.dot(x_v[rows, :], qw_v[...], preferred_element_type=F32).astype(BF16)
        copy = pltpu.make_async_copy(q_v.at[rows], q_out.at[rows], q_sem.at[tile])
        copy.start()
        return copy

    stores = [project(0)]
    for copy in sends:
        copy.wait()
    kvb[...] = (part[pl.ds(y, 1)][0] + rs[0] + rs[1] + rs[2]).astype(BF16)

    half = pl.ds(pl.multiple_of(c * INNER, INNER), INNER)
    other = pl.ds(pl.multiple_of((1 - c) * INNER, INNER), INNER)
    pair = send(kvb.at[:, other], gath.at[x, z, c], pair_s, pair_r, at(y, x, z, 1 - c))
    gath[x, z, c] = kvb[:, half]
    pair.wait()

    first, last = pl.ds(0, INNER // 2), pl.ds(INNER // 2, INNER // 2)
    sends = []
    for k in range(1, NX):
        own = gath.at[x, z, :, :, first]
        sends.append(send(own, own, ag_s.at[0, k], ag_r.at[0, k], at(y, turn(x, k, NX), z, c)))
        own = gath.at[x, z, :, :, last]
        sends.append(send(own, own, ag_s.at[1, k], ag_r.at[1, k], at(y, x, turn(z, k, NZ), c)))
    for copy in sends:
        copy.wait()
    sends = []
    for k in range(1, NX):
        own = gath.at[:, z, :, :, first]
        sends.append(send(own, own, ag_s.at[2, k], ag_r.at[2, k], at(y, x, turn(z, k, NZ), c)))
        own = gath.at[x, :, :, :, last]
        sends.append(send(own, own, ag_s.at[3, k], ag_r.at[3, k], at(y, turn(x, k, NX), z, c)))
    stores.append(project(1))
    stores.append(project(2))
    for copy in sends:
        copy.wait()

    sends = []
    for k in (1, 2, 3, 0):
        for j in range(NC):
            to_y, to_c = turn(y, k, NY), turn(c, j, NC)
            base = (to_y * (NX * NZ * NC) + (x * NZ + z) * NC + to_c) * SAMP
            for i in range(SAMP):
                p = prompt_ref[base + i]
                sel[k, j, i] = gath[lax.div(p, 8), lax.rem(lax.div(p, 2), 4), lax.rem(p, 2)]
            target = kv_out.at[:, y, :, half]
            if k or j:
                sends.append(send(sel.at[k, j], target, sel_s.at[k, j], sel_r.at[k, j], at(to_y, x, z, to_c)))
            else:
                own_copy = pltpu.make_async_copy(sel.at[k, j], target, own_sem)
                own_copy.start()
    stores.append(project(3))
    own_copy.wait()
    for copy in sends:
        copy.wait()
    for copy in stores:
        copy.wait()


def front(sample_prompt, captions, kv_weight, tokens, q_weight):
    any_space = pl.BlockSpec(memory_space=pl.ANY)
    vmem = pl.BlockSpec(memory_space=pltpu.VMEM)
    smem = pl.BlockSpec(memory_space=pltpu.SMEM)
    dma = pltpu.SemaphoreType.DMA
    return pl.pallas_call(
        front_kernel,
        out_shape=(
            jax.ShapeDtypeStruct((SAMP * IMG, INNER), BF16),
            jax.ShapeDtypeStruct((SAMP, NY, TOK, 2 * INNER), BF16),
        ),
        in_specs=[smem, vmem, any_space, any_space, any_space],
        out_specs=(any_space, any_space),
        scratch_shapes=[
            pltpu.VMEM((DEPTH, 2 * INNER), BF16),
            pltpu.VMEM((SAMP * IMG, CIMG), BF16),
            pltpu.VMEM((CIMG, INNER), BF16),
            pltpu.VMEM((SAMP * IMG, INNER), BF16),
            pltpu.VMEM((NY, TOK, DEPTH), BF16),
            pltpu.VMEM((NY, TOK, 2 * INNER), F32),
            pltpu.VMEM((NY - 1, TOK, 2 * INNER), F32),
            pltpu.VMEM((TOK, 2 * INNER), BF16),
            pltpu.VMEM((NX, NZ, NC, TOK, INNER), BF16),
            pltpu.VMEM((NY, NC, SAMP, TOK, INNER), BF16),
            dma((3,)),
            dma((NY,)), dma((NY,)),
            dma((NY, 4)), dma((NY, 4)),
            dma, dma,
            dma((4, NX)), dma((4, NX)),
            dma((NY, NC)), dma((NY, NC)),
            dma,
            dma((SAMP,)),
        ],
        compiler_params=pltpu.CompilerParams(
            collective_id=0, has_side_effects=True, vmem_limit_bytes=VMEM_LIMIT
        ),
    )(sample_prompt, captions, kv_weight, tokens, q_weight)


def attend_kernel(prompt_ref, len_ref, q_ref, grad_ref, kv_ref, qw_ref, context_ref, image_ref, dkv_ref, dq_v):
    grp = lax.axis_index("grp")
    dev = lax.axis_index("dev")
    sample = (grp * (NX * NZ * NC) + dev) * SAMP + pl.program_id(0)
    length = len_ref[prompt_ref[sample]]
    scale = 1.0 / math.sqrt(HD)
    live = lax.broadcasted_iota(jnp.int32, (NY * TOK, IMG), 0) < length
    for h in range(HEADS):
        cols = pl.ds(h * HD, HD)
        vcols = pl.ds(INNER + h * HD, HD)
        q = q_ref[:, cols]
        g = grad_ref[:, cols]
        key = kv_ref[:, cols]
        value = kv_ref[:, vcols]
        nt = (((1,), (1,)), ((), ()))
        tn = (((0,), (0,)), ((), ()))
        scores = lax.dot_general(key, q, nt, preferred_element_type=F32) * scale
        scores = jnp.where(live, scores, NEG_FILL)
        expd = jnp.exp(scores - jnp.max(scores, axis=0, keepdims=True))
        soft = expd * (1.0 / jnp.sum(expd, axis=0, keepdims=True))
        soft_b = soft.astype(BF16)
        d_soft = lax.dot_general(value, g, nt, preferred_element_type=F32)
        inner = jnp.sum(d_soft * soft, axis=0, keepdims=True)
        d_scores = (soft * (d_soft - inner) * scale).astype(BF16)
        context_ref[:, cols] = lax.dot_general(soft_b, value, tn, preferred_element_type=F32).astype(BF16)
        dq_v[:, cols] = lax.dot_general(d_scores, key, tn, preferred_element_type=F32).astype(BF16)
        dkv_ref[:, cols] = jnp.dot(d_scores, q, preferred_element_type=F32).astype(BF16)
        dkv_ref[:, vcols] = jnp.dot(soft_b, g, preferred_element_type=F32).astype(BF16)
    image_ref[...] = lax.dot_general(
        dq_v[...], qw_ref[...], (((1,), (1,)), ((), ())), preferred_element_type=F32
    ).astype(BF16)


def attend(sample_prompt, caption_len, queries, grads, kv, q_weight):
    smem = pl.BlockSpec(memory_space=pltpu.SMEM)
    full = NY * TOK
    return pl.pallas_call(
        attend_kernel,
        grid=(SAMP,),
        out_shape=(
            jax.ShapeDtypeStruct((SAMP, IMG, INNER), BF16),
            jax.ShapeDtypeStruct((SAMP, IMG, CIMG), BF16),
            jax.ShapeDtypeStruct((SAMP, full, 2 * INNER), BF16),
        ),
        in_specs=[
            smem,
            smem,
            pl.BlockSpec((None, IMG, INNER), lambda s: (s, 0, 0)),
            pl.BlockSpec((None, IMG, INNER), lambda s: (s, 0, 0)),
            pl.BlockSpec((None, full, 2 * INNER), lambda s: (s, 0, 0)),
            pl.BlockSpec((CIMG, INNER), lambda s: (0, 0)),
        ],
        out_specs=(
            pl.BlockSpec((None, IMG, INNER), lambda s: (s, 0, 0)),
            pl.BlockSpec((None, IMG, CIMG), lambda s: (s, 0, 0)),
            pl.BlockSpec((None, full, 2 * INNER), lambda s: (s, 0, 0)),
        ),
        scratch_shapes=[pltpu.VMEM((IMG, INNER), BF16)],
        compiler_params=pltpu.CompilerParams(vmem_limit_bytes=VMEM_LIMIT),
    )(sample_prompt, caption_len, queries, grads, kv, q_weight)


def back_kernel(
    prompt_ref, dkv_ref, w_hbm, out_ref,
    w_v, arr, sums, rsb, ra, rb, mid_a, mid_b, ta, tb, kvg, full, cg, cgr,
    load_sem, a_s, a_r, own_sem, r1_s, r1_r, r2_s, r2_r, f_s, f_r, o_s, o_r,
):
    y, x, z, c = place()
    load = pltpu.make_async_copy(w_hbm, w_v, load_sem)
    load.start()
    greet()

    def half_of(core):
        return pl.ds(pl.multiple_of(core * INNER, INNER), INNER)

    sends = []
    for k in (1, 2, 3, 0):
        for j in range(NC):
            to_y, to_c = turn(y, k, NY), turn(c, j, NC)
            piece = dkv_ref.at[:, to_y, :, half_of(to_c)]
            if k or j:
                sends.append(send(piece, arr.at[y, c], a_s.at[k, j], a_r.at[k, j], at(to_y, x, z, to_c)))
            else:
                own_copy = pltpu.make_async_copy(piece, arr.at[y, c], own_sem)
                own_copy.start()

    count = NY * NC * SAMP * TOK
    lanes = lax.broadcasted_iota(jnp.int32, (1, count), 1)
    owner = jnp.zeros((1, count), jnp.int32)
    for yy in range(NY):
        for cc in range(NC):
            for i in range(SAMP):
                spot = (yy * NC + cc) * SAMP + i
                p = prompt_ref[(yy * (NX * NZ * NC) + (x * NZ + z) * NC + cc) * SAMP + i]
                owner = jnp.where(lanes // TOK == spot, p, owner)
    wanted = owner * TOK + lanes % TOK
    rows = lax.broadcasted_iota(jnp.int32, (PROMPTS * TOK, count), 0)
    match = jnp.where(rows == wanted, 1.0, 0.0).astype(BF16)
    own_copy.wait()
    for copy in sends:
        copy.wait()
    total = jnp.dot(match, arr[...].reshape(count, INNER), preferred_element_type=F32)
    total = total.reshape(NX, NZ, NC, TOK, INNER)
    sums[...] = total
    rsb[...] = total.astype(BF16)

    first, last = pl.ds(0, INNER // 2), pl.ds(INNER // 2, INNER // 2)
    sends = []
    for k in range(1, NX):
        to = turn(x, k, NX)
        sends.append(send(rsb.at[to, :, :, :, first], ra.at[k - 1], r1_s.at[0, k], r1_r.at[0, k], at(y, to, z, c)))
        to = turn(z, k, NZ)
        sends.append(send(rsb.at[:, to, :, :, last], rb.at[k - 1], r1_s.at[1, k], r1_r.at[1, k], at(y, x, to, c)))
    for copy in sends:
        copy.wait()
    mid_a[...] = sums[x, :, :, :, first] + ra[0].astype(F32) + ra[1].astype(F32) + ra[2].astype(F32)
    for xx in range(NX):
        mid_b[xx] = sums[xx, z, :, :, last] + rb[0, xx].astype(F32) + rb[1, xx].astype(F32) + rb[2, xx].astype(F32)
    sends = []
    for k in range(1, NX):
        to = turn(z, k, NZ)
        sends.append(send(mid_a.at[to], ta.at[k - 1], r2_s.at[0, k], r2_r.at[0, k], at(y, x, to, c)))
        to = turn(x, k, NX)
        sends.append(send(mid_b.at[to], tb.at[k - 1], r2_s.at[1, k], r2_r.at[1, k], at(y, to, z, c)))
    for copy in sends:
        copy.wait()
    kvg[:, :, first] = (mid_a[z] + ta[0] + ta[1] + ta[2]).astype(BF16)
    kvg[:, :, last] = (mid_b[x] + tb[0] + tb[1] + tb[2]).astype(BF16)

    sends = []
    for k in range(NY):
        for j in range(NC):
            to_y, to_c = turn(y, k, NY), turn(c, j, NC)
            if k or j:
                sends.append(
                    send(kvg.at[to_c], full.at[y, :, half_of(c)], f_s.at[k, j], f_r.at[k, j], at(to_y, x, z, to_c))
                )
    full[y, :, half_of(c)] = kvg[c]
    load.wait()
    for copy in sends:
        copy.wait()
    cg[...] = lax.dot_general(
        full[...].reshape(NY * TOK, 2 * INNER), w_v[...], (((1,), (1,)), ((), ())), preferred_element_type=F32
    ).reshape(NY, TOK, DEPTH)
    sends = []
    for k in range(1, NY):
        to = turn(y, k, NY)
        sends.append(send(cg.at[to], cgr.at[y], o_s.at[k], o_r.at[k], at(to, x, z, c)))
    cgr[y] = cg[y]
    for copy in sends:
        copy.wait()
    for yy in range(NY):
        out_ref[:, pl.ds(yy * DEPTH, DEPTH)] = cgr[yy]


def back(sample_prompt, dkv, kv_weight):
    any_space = pl.BlockSpec(memory_space=pl.ANY)
    vmem = pl.BlockSpec(memory_space=pltpu.VMEM)
    smem = pl.BlockSpec(memory_space=pltpu.SMEM)
    dma = pltpu.SemaphoreType.DMA
    return pl.pallas_call(
        back_kernel,
        out_shape=jax.ShapeDtypeStruct((TOK, WIDE), F32),
        in_specs=[smem, any_space, any_space],
        out_specs=vmem,
        scratch_shapes=[
            pltpu.VMEM((DEPTH, 2 * INNER), BF16),
            pltpu.VMEM((NY, NC, SAMP, TOK, INNER), BF16),
            pltpu.VMEM((NX, NZ, NC, TOK, INNER), F32),
            pltpu.VMEM((NX, NZ, NC, TOK, INNER), BF16),
            pltpu.VMEM((NX - 1, NZ, NC, TOK, INNER // 2), BF16),
            pltpu.VMEM((NZ - 1, NX, NC, TOK, INNER // 2), BF16),
            pltpu.VMEM((NZ, NC, TOK, INNER // 2), F32),
            pltpu.VMEM((NX, NC, TOK, INNER // 2), F32),
            pltpu.VMEM((NZ - 1, NC, TOK, INNER // 2), F32),
            pltpu.VMEM((NX - 1, NC, TOK, INNER // 2), F32),
            pltpu.VMEM((NC, TOK, INNER), BF16),
            pltpu.VMEM((NY, TOK, 2 * INNER), BF16),
            pltpu.VMEM((NY, TOK, DEPTH), F32),
            pltpu.VMEM((NY, TOK, DEPTH), F32),
            dma,
            dma((NY, NC)), dma((NY, NC)),
            dma,
            dma((2, NX)), dma((2, NX)),
            dma((2, NX)), dma((2, NX)),
            dma((NY, NC)), dma((NY, NC)),
            dma((NY,)), dma((NY,)),
        ],
        compiler_params=pltpu.CompilerParams(
            collective_id=1, has_side_effects=True, vmem_limit_bytes=VMEM_LIMIT
        ),
    )(sample_prompt, dkv, kv_weight)


def shards(captions, kv_weight, image_tokens, q_weight, context_grad, sample_prompt, caption_len):
    queries, kv = front(
        sample_prompt,
        captions.reshape(TOK, WIDE),
        kv_weight,
        image_tokens.reshape(SAMP * IMG, CIMG),
        q_weight,
    )
    context, image_grad, dkv = attend(
        sample_prompt,
        caption_len,
        queries.reshape(SAMP, IMG, INNER),
        context_grad,
        kv.reshape(SAMP, NY * TOK, 2 * INNER),
        q_weight,
    )
    caption_grad = back(sample_prompt, dkv.reshape(SAMP, NY, TOK, 2 * INNER), kv_weight)
    return context, image_grad, caption_grad.reshape(1, TOK, WIDE)


def solution(mesh):
    placed = (
        P("dev", "grp", None),
        P("grp", None),
        P(("grp", "dev"), None, None),
        P(),
        P(("grp", "dev"), None, None),
        P(),
        P(),
    )
    return jax.shard_map(
        shards,
        mesh=mesh,
        in_specs=placed,
        out_specs=(
            P(("grp", "dev"), None, None),
            P(("grp", "dev"), None, None),
            P("dev", "grp", None),
        ),
        check_vma=False,
    )
```

```python
import math

import jax
import jax.numpy as jnp
from jax import lax
from jax.experimental import pallas as pl
from jax.experimental.pallas import tpu as pltpu
from jax.sharding import PartitionSpec as P

HEADS = 8
HD = 128
NEG_FILL = -1e30
MESH = pl.DeviceIdType.MESH
BF16 = jnp.bfloat16
F32 = jnp.float32
VMEM_LIMIT = 56 * 1024 * 1024

NY, NX, NZ, NC = 4, 4, 4, 2
SAMP = 4
TOK = 16
INNER = 1024
WIDE = 4096
DEPTH = 1024
IMG = 256
CIMG = 2048
PROMPTS = 32
CHUNKS = 4
CW = INNER // CHUNKS
NT = (((1,), (1,)), ((), ()))
TN = (((0,), (0,)), ((), ()))


def place():
    grp = lax.axis_index("grp")
    dev = lax.axis_index("dev")
    return grp, lax.div(dev, 8), lax.rem(lax.div(dev, 2), 4), lax.rem(dev, 2)


def at(grp, x, z, core):
    return {"grp": grp, "dev": (x * NZ + z) * NC + core}


def turn(index, step, size):
    return lax.rem(index + step, size)


def greet():
    y, x, z, c = place()
    barrier = pltpu.get_barrier_semaphore()
    peers = [at(turn(y, k, NY), x, z, turn(c, j, NC)) for k in range(NY) for j in range(NC) if k or j]
    peers += [at(y, turn(x, k, NX), z, c) for k in range(1, NX)]
    peers += [at(y, x, turn(z, k, NZ), c) for k in range(1, NZ)]
    for peer in peers:
        pl.semaphore_signal(barrier, inc=1, device_id=peer, device_id_type=MESH)
    pl.semaphore_wait(barrier, len(peers))


def send(src, dst, send_sem, recv_sem, peer):
    copy = pltpu.make_async_remote_copy(
        src_ref=src, dst_ref=dst, send_sem=send_sem, recv_sem=recv_sem, device_id=peer, device_id_type=MESH
    )
    copy.start()
    return copy


def kernel(
    prompt_ref, len_ref, cap_hbm, w_hbm, x_hbm, qw_hbm, g_hbm, context_out, image_out, caption_out, *scratch
):
    (
        w_v, x_v, qw_v, q_v, g_v, ctx_v, dq_v, caps, part, rs, kvb, sel, skv, dkv, arr, match,
        sums, rsb, r1, mid, r2, kvg, full, cg,
        load_sem, cap_s, cap_r, rs_s, rs_r, pair_s, pair_r, ag_s, ag_r, sel_s, sel_r,
        grad_s, grad_r, r1_s, r1_r, r2_s, r2_r, f_s, f_r, o_s, o_r, store_sem,
    ) = scratch[:-CHUNKS]
    gath = scratch[-CHUNKS:]
    y, x, z, c = place()
    waits = []

    def push(src, dst, send_sem, recv_sem, peer):
        copy = send(src, dst, send_sem, recv_sem, peer)
        waits.append(copy.wait_send)
        return copy

    def columns(index):
        return pl.ds(pl.multiple_of(index * DEPTH, DEPTH), DEPTH)

    def keep(src, dst, sem):
        copy = pltpu.make_async_copy(src, dst, sem)
        copy.start()
        return copy

    own_cap = keep(cap_hbm.at[:, columns(y)], caps.at[y], load_sem.at[0])
    load_w = keep(w_hbm, w_v, load_sem.at[1])
    load_x = keep(x_hbm, x_v, load_sem.at[2])
    load_qw = keep(qw_hbm, qw_v, load_sem.at[3])
    load_g = keep(g_hbm, g_v, load_sem.at[4])
    greet()

    def project(tile):
        rows = pl.ds(tile * IMG, IMG)
        q_v[rows, :] = jnp.dot(x_v[rows, :], qw_v[...], preferred_element_type=F32).astype(BF16)

    arrive = []
    for k in range(1, NY):
        to = turn(y, k, NY)
        arrive.append(push(cap_hbm.at[:, columns(to)], caps.at[y], cap_s.at[k], cap_r.at[k], at(to, x, z, c)))
    load_x.wait()
    load_qw.wait()
    project(0)
    own_cap.wait()
    load_w.wait()
    for copy in arrive:
        copy.wait_recv()

    rs_copies = []
    for q in range(CHUNKS):
        lhs = caps[...].reshape(NY * TOK, DEPTH)
        for half in range(2):
            part[q, :, :, pl.ds(half * CW, CW)] = jnp.dot(
                lhs, w_v[:, pl.ds(half * INNER + q * CW, CW)], preferred_element_type=F32
            ).reshape(NY, TOK, CW)
        copies = []
        for k in range(1, NY):
            to = turn(y, k, NY)
            copies.append(push(part.at[q, to], rs.at[q, k - 1], rs_s.at[q, k], rs_r.at[q, k], at(to, x, z, c)))
        rs_copies.append(copies)
    project(1)

    pair_copies = []
    for q in range(CHUNKS):
        for copy in rs_copies[q]:
            copy.wait_recv()
        whole = (part[q, y] + rs[q, 0] + rs[q, 1] + rs[q, 2]).astype(BF16)
        kvb[q, 0] = whole[:, :CW]
        kvb[q, 1] = whole[:, CW:]
        pair_copies.append(
            push(kvb.at[q, 1 - c], gath[q].at[x, z, c], pair_s.at[q], pair_r.at[q], at(y, x, z, 1 - c))
        )
        gath[q][x, z, c] = kvb[q, c]

    def over(axis, k):
        return (turn(x, k, NX), at(y, turn(x, k, NX), z, c)) if axis == 0 else (
            turn(z, k, NZ), at(y, x, turn(z, k, NZ), c))

    first_copies = []
    for q in range(CHUNKS):
        pair_copies[q].wait_recv()
        own = gath[q].at[x, z]
        first_copies.append(
            [push(own, own, ag_s.at[0, q, k], ag_r.at[0, q, k], over(q % 2, k)[1]) for k in range(1, NX)]
        )
    project(2)
    second_copies = []
    for q in range(CHUNKS):
        for copy in first_copies[q]:
            copy.wait_recv()
        own = gath[q].at[:, z] if q % 2 == 0 else gath[q].at[x]
        second_copies.append(
            [push(own, own, ag_s.at[1, q, k], ag_r.at[1, q, k], over(1 - q % 2, k)[1]) for k in range(1, NX)]
        )
    project(3)

    sel_copies = []
    for q in range(CHUNKS):
        for copy in second_copies[q]:
            copy.wait_recv()
        copies = []
        for k in (2, 1, 3, 0):
            for j in range(NC):
                to_y, to_c = turn(y, k, NY), turn(c, j, NC)
                base = (to_y * (NX * NZ * NC) + (x * NZ + z) * NC + to_c) * SAMP
                for i in range(SAMP):
                    p = prompt_ref[base + i]
                    block = gath[q][lax.div(p, 8), lax.rem(lax.div(p, 2), 4), lax.rem(p, 2)]
                    if k or j:
                        sel[q, k, j, i] = block
                    else:
                        skv[q, c, i, y] = block
                if k or j:
                    copies.append(
                        push(
                            sel.at[q, k, j], skv.at[q, c, :, y], sel_s.at[q, k, j], sel_r.at[q, k, j],
                            at(to_y, x, z, to_c),
                        )
                    )
        sel_copies.append(copies)
    load_g.wait()

    count = NY * NC * SAMP * TOK
    lanes = lax.broadcasted_iota(jnp.int32, (1, count), 1)
    owner = jnp.zeros((1, count), jnp.int32)
    for yy in range(NY):
        for cc in range(NC):
            for i in range(SAMP):
                spot = (yy * NC + cc) * SAMP + i
                p = prompt_ref[(yy * (NX * NZ * NC) + (x * NZ + z) * NC + cc) * SAMP + i]
                owner = jnp.where(lanes // TOK == spot, p, owner)
    wanted = owner * TOK + lanes % TOK
    ids = lax.broadcasted_iota(jnp.int32, (PROMPTS * TOK, count), 0)
    match[...] = jnp.where(ids == wanted, 1.0, 0.0).astype(BF16)

    scale = 1.0 / math.sqrt(HD)
    base = (y * (NX * NZ * NC) + (x * NZ + z) * NC + c) * SAMP
    tokens = NY * TOK

    def attention(q, s):
        rows = pl.ds(pl.multiple_of(s * IMG, IMG), IMG)
        cols = pl.ds(q * CW, CW)
        length = len_ref[prompt_ref[base + s]]
        live = lax.broadcasted_iota(jnp.int32, (2, tokens, IMG), 1) < length
        lead = lax.broadcasted_iota(jnp.int32, (tokens, CW), 1) < HD
        queries = q_v[rows, cols]
        grads = g_v[rows, cols]
        key = skv[q, 0, s].reshape(tokens, CW)
        value = skv[q, 1, s].reshape(tokens, CW)
        zero = jnp.zeros_like(key)
        key2 = jnp.concatenate([jnp.where(lead, key, zero), jnp.where(lead, zero, key)], axis=0)
        value2 = jnp.concatenate([jnp.where(lead, value, zero), jnp.where(lead, zero, value)], axis=0)
        scores = lax.dot_general(key2, queries, NT, preferred_element_type=F32) * scale
        scores = jnp.where(live, scores.reshape(2, tokens, IMG), NEG_FILL)
        expd = jnp.exp(scores - jnp.max(scores, axis=1, keepdims=True))
        soft = expd * (1.0 / jnp.sum(expd, axis=1, keepdims=True))
        soft_b = soft.astype(BF16).reshape(2 * tokens, IMG)
        d_soft = lax.dot_general(value2, grads, NT, preferred_element_type=F32).reshape(2, tokens, IMG)
        inner = jnp.sum(d_soft * soft, axis=1, keepdims=True)
        d_scores = (soft * (d_soft - inner) * scale).astype(BF16).reshape(2 * tokens, IMG)
        ctx_v[rows, cols] = lax.dot_general(soft_b, value2, TN, preferred_element_type=F32).astype(BF16)
        dq_v[rows, cols] = lax.dot_general(d_scores, key2, TN, preferred_element_type=F32).astype(BF16)
        d_key = jnp.dot(d_scores, queries, preferred_element_type=F32)
        d_value = jnp.dot(soft_b, grads, preferred_element_type=F32)
        dkv[q, 0, s] = jnp.where(lead, d_key[:tokens], d_key[tokens:]).astype(BF16).reshape(NY, TOK, CW)
        dkv[q, 1, s] = jnp.where(lead, d_value[:tokens], d_value[tokens:]).astype(BF16).reshape(NY, TOK, CW)

    grad_copies, r1_copies, r2_copies, f_copies = {}, {}, {}, {}

    def attend(q):
        for copy in sel_copies[q]:
            copy.wait_recv()

        def two(t, carry):
            attention(q, 2 * t)
            attention(q, 2 * t + 1)
            return carry

        lax.fori_loop(0, SAMP // 2, two, 0)
        copies = []
        for k in (2, 1, 3, 0):
            for j in range(NC):
                to_y, to_c = turn(y, k, NY), turn(c, j, NC)
                if k or j:
                    copies.append(
                        push(
                            dkv.at[q, to_c, :, to_y], arr.at[q, y, c], grad_s.at[q, k, j], grad_r.at[q, k, j],
                            at(to_y, x, z, to_c),
                        )
                    )
        arr[q, y, c] = dkv[q, c, :, y]
        grad_copies[q] = copies
        cols = pl.ds(q * CW, CW)
        waits.append(keep(ctx_v.at[:, cols], context_out.at[:, cols], store_sem.at[q]).wait)

    def add_up(q):
        for copy in grad_copies[q]:
            copy.wait_recv()
        total = jnp.dot(match[...], arr[q].reshape(count, CW), preferred_element_type=F32)
        total = total.reshape(NX, NZ, NC, TOK, CW)
        sums[q] = total
        rsb[q] = total.astype(BF16)
        copies = []
        for k in range(1, NX):
            to, peer = over(q % 2, k)
            piece = rsb.at[q, to] if q % 2 == 0 else rsb.at[q, :, to]
            copies.append(push(piece, r1.at[q, k - 1], r1_s.at[q, k], r1_r.at[q, k], peer))
        r1_copies[q] = copies

    def scatter(q):
        for copy in r1_copies[q]:
            copy.wait_recv()
        own = sums[q, x] if q % 2 == 0 else sums[q, :, z]
        mid[q] = own + r1[q, 0].astype(F32) + r1[q, 1].astype(F32) + r1[q, 2].astype(F32)
        copies = []
        for k in range(1, NX):
            to, peer = over(1 - q % 2, k)
            copies.append(push(mid.at[q, to], r2.at[q, k - 1], r2_s.at[q, k], r2_r.at[q, k], peer))
        r2_copies[q] = copies

    def spread(q):
        for copy in r2_copies[q]:
            copy.wait_recv()
        own = mid[q, z] if q % 2 == 0 else mid[q, x]
        kvg[q] = (own + r2[q, 0] + r2[q, 1] + r2[q, 2]).astype(BF16)
        copies = []
        for k in (2, 1, 3, 0):
            for j in range(NC):
                to_y, to_c = turn(y, k, NY), turn(c, j, NC)
                if k or j:
                    copies.append(
                        push(
                            kvg.at[q, to_c], full.at[q, c, y], f_s.at[q, k, j], f_r.at[q, k, j],
                            at(to_y, x, z, to_c),
                        )
                    )
        full[q, c, y] = kvg[q, c]
        f_copies[q] = copies

    def finish(q):
        for copy in f_copies[q]:
            copy.wait_recv()
        term = None
        for half in range(2):
            more = lax.dot_general(
                full[q, half].reshape(tokens, CW), w_v[:, pl.ds(half * INNER + q * CW, CW)], NT,
                preferred_element_type=F32,
            )
            term = more if term is None else term + more
        term = term.reshape(NY, TOK, DEPTH)
        cg[...] = term if q == 0 else cg[...] + term

    def image(tile):
        rows = pl.ds(tile * IMG, IMG)
        x_v[rows, :] = lax.dot_general(dq_v[rows, :], qw_v[...], NT, preferred_element_type=F32).astype(BF16)
        waits.append(keep(x_v.at[rows], image_out.at[rows], store_sem.at[CHUNKS + tile]).wait)

    attend(0)
    attend(1)
    add_up(0)
    attend(2)
    add_up(1)
    scatter(0)
    attend(3)
    add_up(2)
    scatter(1)
    spread(0)
    image(0)
    add_up(3)
    scatter(2)
    spread(1)
    finish(0)
    image(1)
    scatter(3)
    spread(2)
    finish(1)
    image(2)
    spread(3)
    finish(2)
    image(3)
    finish(3)
    arrive = []
    for k in range(1, NY):
        to = turn(y, k, NY)
        arrive.append(push(cg.at[to], caption_out.at[:, columns(y)], o_s.at[k], o_r.at[k], at(to, x, z, c)))
    waits.append(keep(cg.at[y], caption_out.at[:, columns(y)], store_sem.at[CHUNKS + SAMP]).wait)
    for copy in arrive:
        copy.wait_recv()
    for wait in waits:
        wait()


def shards(captions, kv_weight, image_tokens, q_weight, context_grad, sample_prompt, caption_len):
    any_space = pl.BlockSpec(memory_space=pl.ANY)
    smem = pl.BlockSpec(memory_space=pltpu.SMEM)
    dma = pltpu.SemaphoreType.DMA
    rows = SAMP * IMG

    def pair(*shape):
        return [dma(shape), dma(shape)]

    context, image_grad, caption_grad = pl.pallas_call(
        kernel,
        out_shape=(
            jax.ShapeDtypeStruct((rows, INNER), BF16),
            jax.ShapeDtypeStruct((rows, CIMG), BF16),
            jax.ShapeDtypeStruct((TOK, WIDE), F32),
        ),
        in_specs=[smem, smem] + [any_space] * 5,
        out_specs=(any_space,) * 3,
        scratch_shapes=[
            pltpu.VMEM((DEPTH, 2 * INNER), BF16),
            pltpu.VMEM((rows, CIMG), BF16),
            pltpu.VMEM((CIMG, INNER), BF16),
            pltpu.VMEM((rows, INNER), BF16),
            pltpu.VMEM((rows, INNER), BF16),
            pltpu.VMEM((rows, INNER), BF16),
            pltpu.VMEM((rows, INNER), BF16),
            pltpu.VMEM((NY, TOK, DEPTH), BF16),
            pltpu.VMEM((CHUNKS, NY, TOK, 2 * CW), F32),
            pltpu.VMEM((CHUNKS, NY - 1, TOK, 2 * CW), F32),
            pltpu.VMEM((CHUNKS, 2, TOK, CW), BF16),
            pltpu.VMEM((CHUNKS, NY, NC, SAMP, TOK, CW), BF16),
            pltpu.VMEM((CHUNKS, 2, SAMP, NY, TOK, CW), BF16),
            pltpu.VMEM((CHUNKS, 2, SAMP, NY, TOK, CW), BF16),
            pltpu.VMEM((CHUNKS, NY, NC, SAMP, TOK, CW), BF16),
            pltpu.VMEM((PROMPTS * TOK, NY * NC * SAMP * TOK), BF16),
            pltpu.VMEM((CHUNKS, NX, NZ, NC, TOK, CW), F32),
            pltpu.VMEM((CHUNKS, NX, NZ, NC, TOK, CW), BF16),
            pltpu.VMEM((CHUNKS, NX - 1, NZ, NC, TOK, CW), BF16),
            pltpu.VMEM((CHUNKS, NZ, NC, TOK, CW), F32),
            pltpu.VMEM((CHUNKS, NZ - 1, NC, TOK, CW), F32),
            pltpu.VMEM((CHUNKS, NC, TOK, CW), BF16),
            pltpu.VMEM((CHUNKS, 2, NY, TOK, CW), BF16),
            pltpu.VMEM((NY, TOK, DEPTH), F32),
            dma((5,)),
            *pair(NY),
            *pair(CHUNKS, NY),
            *pair(CHUNKS),
            *pair(2, CHUNKS, NX),
            *pair(CHUNKS, NY, NC),
            *pair(CHUNKS, NY, NC),
            *pair(CHUNKS, NX),
            *pair(CHUNKS, NX),
            *pair(CHUNKS, NY, NC),
            *pair(NY),
            dma((CHUNKS + SAMP + 1,)),
        ] + [pltpu.VMEM((NX, NZ, NC, TOK, CW), BF16) for _ in range(CHUNKS)],
        compiler_params=pltpu.CompilerParams(
            collective_id=0, has_side_effects=True, vmem_limit_bytes=VMEM_LIMIT
        ),
    )(
        sample_prompt,
        caption_len,
        captions.reshape(TOK, WIDE),
        kv_weight,
        image_tokens.reshape(rows, CIMG),
        q_weight,
        context_grad.reshape(rows, INNER),
    )
    return (
        context.reshape(SAMP, IMG, INNER),
        image_grad.reshape(SAMP, IMG, CIMG),
        caption_grad.reshape(1, TOK, WIDE),
    )


def solution(mesh):
    placed = (
        P("dev", "grp", None),
        P("grp", None),
        P(("grp", "dev"), None, None),
        P(),
        P(("grp", "dev"), None, None),
        P(),
        P(),
    )
    return jax.shard_map(
        shards,
        mesh=mesh,
        in_specs=placed,
        out_specs=(
            P(("grp", "dev"), None, None),
            P(("grp", "dev"), None, None),
            P("dev", "grp", None),
        ),
        check_vma=False,
    )
```

```python
import math

import jax
import jax.numpy as jnp
from jax import lax
from jax.experimental import pallas as pl
from jax.experimental.pallas import tpu as pltpu
from jax.sharding import PartitionSpec as P

HEADS = 8
HD = 128
NEG_FILL = -1e30
MESH = pl.DeviceIdType.MESH
BF16 = jnp.bfloat16
F32 = jnp.float32
VMEM_LIMIT = 56 * 1024 * 1024

NY, NX, NZ, NC = 4, 4, 4, 2
SAMP = 4
TOK = 16
INNER = 1024
WIDE = 4096
DEPTH = 1024
IMG = 256
CIMG = 2048
PROMPTS = 32
CHUNKS = 4
CW = INNER // CHUNKS
LINE = [(k, j) for k in (2, 1, 3, 0) for j in (1, 0)]
NT = (((1,), (1,)), ((), ()))
TN = (((0,), (0,)), ((), ()))


def place():
    grp = lax.axis_index("grp")
    dev = lax.axis_index("dev")
    return grp, lax.div(dev, 8), lax.rem(lax.div(dev, 2), 4), lax.rem(dev, 2)


def at(grp, x, z, core):
    return {"grp": grp, "dev": (x * NZ + z) * NC + core}


def turn(index, step, size):
    return lax.rem(index + step, size)


def greet():
    y, x, z, c = place()
    barrier = pltpu.get_barrier_semaphore()
    peers = [at(turn(y, k, NY), x, z, turn(c, j, NC)) for k in range(1, NY) for j in range(NC)]
    peers += [
        at(y, turn(x, i, NX), turn(z, j, NZ), turn(c, k, NC))
        for i in range(NX) for j in range(NZ) for k in range(NC) if i or j or k
    ]
    for peer in peers:
        pl.semaphore_signal(barrier, inc=1, device_id=peer, device_id_type=MESH)
    pl.semaphore_wait(barrier, len(peers))


def send(src, dst, send_sem, recv_sem, peer):
    pltpu.make_async_remote_copy(
        src_ref=src, dst_ref=dst, send_sem=send_sem, recv_sem=recv_sem, device_id=peer, device_id_type=MESH
    ).start()


def take(sem, like):
    pltpu.make_async_copy(like, like, sem).wait()


def kernel(
    prompt_ref, len_ref, cap_hbm, w_hbm, x_hbm, qw_hbm, g_hbm, context_out, image_out, caption_out, *scratch
):
    (
        w_v, x_v, qw_v, q_v, g_v, ctx_v, dq_v, caps, part, rs, kvb, sel, skv, dkv, arr, match,
        sums, rsb, r1, kvg, full, cg,
        load_sem, sent, cap_r, rs_r, ag_r, sel_r, grad_r, r1_r, f_r, o_r, store_sem,
    ) = scratch[:-CHUNKS]
    gath = scratch[-CHUNKS:]
    y, x, z, c = place()
    stores = []

    def columns(index):
        return pl.ds(pl.multiple_of(index * DEPTH, DEPTH), DEPTH)

    def keep(src, dst, sem):
        copy = pltpu.make_async_copy(src, dst, sem)
        copy.start()
        return copy

    own_cap = keep(cap_hbm.at[:, columns(y)], caps.at[y], load_sem.at[0])
    load_w = keep(w_hbm, w_v, load_sem.at[1])
    load_qw = keep(qw_hbm, qw_v, load_sem.at[3])
    load_x = keep(x_hbm, x_v, load_sem.at[2])
    greet()

    for k in (2, 1, 3):
        to = turn(y, k, NY)
        send(cap_hbm.at[:, columns(to)], caps.at[y], sent.at[0], cap_r, at(to, x, z, c))
    own_cap.wait()
    load_w.wait()
    take(cap_r, caps.at[pl.ds(0, NY - 1)])
    load_g = keep(g_hbm, g_v, load_sem.at[4])

    def project(tile):
        rows = pl.ds(tile * IMG, IMG)
        q_v[rows, :] = jnp.dot(x_v[rows, :], qw_v[...], preferred_element_type=F32).astype(BF16)

    def partial(q):
        lhs = caps[...].reshape(NY * TOK, DEPTH)
        for half in range(2):
            part[q, :, :, pl.ds(half * CW, CW)] = jnp.dot(
                lhs, w_v[:, pl.ds(half * INNER + q * CW, CW)], preferred_element_type=F32
            ).reshape(NY, TOK, CW)
        for k in (2, 1, 3):
            to = turn(y, k, NY)
            send(part.at[q, to], rs.at[q, k - 1], sent.at[1], rs_r.at[q], at(to, x, z, c))

    me = (x * NZ + z) * NC + c

    def gather(q):
        take(rs_r.at[q], rs.at[q])
        whole = (part[q, y] + rs[q, 0] + rs[q, 1] + rs[q, 2]).astype(BF16)
        kvb[q, 0] = whole[:, :CW]
        kvb[q, 1] = whole[:, CW:]
        for i in (2, 1, 3, 0):
            for j in (2, 1, 3, 0):
                for k in range(NC):
                    if i or j or k:
                        to_c = turn(c, k, NC)
                        send(
                            kvb.at[q, to_c], gath[q].at[me], sent.at[2], ag_r.at[q],
                            at(y, turn(x, i, NX), turn(z, j, NZ), to_c),
                        )
        gath[q][me] = kvb[q, c]

    def select(q):
        take(ag_r.at[q], gath[q].at[pl.ds(0, PROMPTS - 1)])
        for slot, (k, j) in enumerate(LINE):
            to_y, to_c = turn(y, k, NY), turn(c, j, NC)
            start = (to_y * (NX * NZ * NC) + (x * NZ + z) * NC + to_c) * SAMP
            for i in range(SAMP):
                block = gath[q][prompt_ref[start + i]]
                if k or j:
                    sel[q, slot * SAMP + i] = block
                else:
                    skv[q, c, i, y] = block
            if k or j:
                send(sel.at[q, pl.ds(slot * SAMP, SAMP)], skv.at[q, c, :, y], sent.at[3], sel_r.at[q], at(to_y, x, z, to_c))

    count = NY * NC * SAMP * TOK

    def one_hot():
        lanes = lax.broadcasted_iota(jnp.int32, (1, count), 1)
        owner = jnp.zeros((1, count), jnp.int32)
        for yy in range(NY):
            for cc in range(NC):
                for i in range(SAMP):
                    spot = (yy * NC + cc) * SAMP + i
                    p = prompt_ref[(yy * (NX * NZ * NC) + (x * NZ + z) * NC + cc) * SAMP + i]
                    owner = jnp.where(lanes // TOK == spot, p, owner)
        wanted = owner * TOK + lanes % TOK
        ids = lax.broadcasted_iota(jnp.int32, (PROMPTS * TOK, count), 0)
        match[...] = jnp.where(ids == wanted, 1.0, 0.0).astype(BF16)

    partial(0)
    partial(1)
    partial(2)
    partial(3)
    load_qw.wait()
    load_x.wait()
    project(0)
    gather(0)
    gather(1)
    gather(2)
    project(1)
    gather(3)
    project(2)
    select(0)
    project(3)
    select(1)
    select(2)
    select(3)
    one_hot()
    load_g.wait()

    scale = 1.0 / math.sqrt(HD)
    base = (y * (NX * NZ * NC) + (x * NZ + z) * NC + c) * SAMP
    tokens = NY * TOK

    def attention(q, s):
        rows = pl.ds(pl.multiple_of(s * IMG, IMG), IMG)
        cols = pl.ds(q * CW, CW)
        length = len_ref[prompt_ref[base + s]]
        live = lax.broadcasted_iota(jnp.int32, (2, tokens, IMG), 1) < length
        lead = lax.broadcasted_iota(jnp.int32, (tokens, CW), 1) < HD
        queries = q_v[rows, cols]
        grads = g_v[rows, cols]
        key = skv[q, 0, s].reshape(tokens, CW)
        value = skv[q, 1, s].reshape(tokens, CW)
        zero = jnp.zeros_like(key)
        key2 = jnp.concatenate([jnp.where(lead, key, zero), jnp.where(lead, zero, key)], axis=0)
        value2 = jnp.concatenate([jnp.where(lead, value, zero), jnp.where(lead, zero, value)], axis=0)
        scores = lax.dot_general(key2, queries, NT, preferred_element_type=F32) * scale
        scores = jnp.where(live, scores.reshape(2, tokens, IMG), NEG_FILL)
        expd = jnp.exp(scores - jnp.max(scores, axis=1, keepdims=True))
        soft = expd * (1.0 / jnp.sum(expd, axis=1, keepdims=True))
        soft_b = soft.astype(BF16).reshape(2 * tokens, IMG)
        d_soft = lax.dot_general(value2, grads, NT, preferred_element_type=F32).reshape(2, tokens, IMG)
        inner = jnp.sum(d_soft * soft, axis=1, keepdims=True)
        d_scores = (soft * (d_soft - inner) * scale).astype(BF16).reshape(2 * tokens, IMG)
        ctx_v[rows, cols] = lax.dot_general(soft_b, value2, TN, preferred_element_type=F32).astype(BF16)
        dq_v[rows, cols] = lax.dot_general(d_scores, key2, TN, preferred_element_type=F32).astype(BF16)
        d_key = jnp.dot(d_scores, queries, preferred_element_type=F32)
        d_value = jnp.dot(soft_b, grads, preferred_element_type=F32)
        dkv[q, 0, s] = jnp.where(lead, d_key[:tokens], d_key[tokens:]).astype(BF16).reshape(NY, TOK, CW)
        dkv[q, 1, s] = jnp.where(lead, d_value[:tokens], d_value[tokens:]).astype(BF16).reshape(NY, TOK, CW)

    seven = pl.ds(0, (NY * NC - 1) * SAMP)

    def attend(q):
        take(sel_r.at[q], sel.at[q, seven])

        def two(t, carry):
            attention(q, 2 * t)
            attention(q, 2 * t + 1)
            return carry

        lax.fori_loop(0, SAMP // 2, two, 0)
        for k, j in LINE[:-1]:
            to_y, to_c = turn(y, k, NY), turn(c, j, NC)
            send(dkv.at[q, to_c, :, to_y], arr.at[q, y, c], sent.at[4], grad_r.at[q], at(to_y, x, z, to_c))
        arr[q, y, c] = dkv[q, c, :, y]
        cols = pl.ds(q * CW, CW)
        stores.append(keep(ctx_v.at[:, cols], context_out.at[:, cols], store_sem.at[q]))

    def add_up(q):
        take(grad_r.at[q], sel.at[q, seven])
        total = jnp.dot(match[...], arr[q].reshape(count, CW), preferred_element_type=F32)
        total = total.reshape(NX, NZ, NC, TOK, CW)
        sums[q] = total
        rsb[q] = total.astype(BF16)
        for i in (2, 1, 3, 0):
            for j in (2, 1, 3, 0):
                if i or j:
                    to_x, to_z = turn(x, i, NX), turn(z, j, NZ)
                    send(
                        rsb.at[q, to_x, to_z], r1.at[q, i * NZ + j - 1], sent.at[5], r1_r.at[q],
                        at(y, to_x, to_z, c),
                    )

    def spread(q):
        take(r1_r.at[q], r1.at[q])
        own = sums[q, x, z]
        for slot in range(NX * NZ - 1):
            own = own + r1[q, slot].astype(F32)
        kvg[q] = own.astype(BF16)
        for k, j in LINE[:-1]:
            to_y, to_c = turn(y, k, NY), turn(c, j, NC)
            send(kvg.at[q, to_c], full.at[q, c, y], sent.at[6], f_r.at[q], at(to_y, x, z, to_c))
        full[q, c, y] = kvg[q, c]

    def finish(q):
        take(f_r.at[q], gath[q].at[pl.ds(0, NY * NC - 1)])
        term = None
        for half in range(2):
            more = lax.dot_general(
                full[q, half].reshape(tokens, CW), w_v[:, pl.ds(half * INNER + q * CW, CW)], NT,
                preferred_element_type=F32,
            )
            term = more if term is None else term + more
        term = term.reshape(NY, TOK, DEPTH)
        cg[...] = term if q == 0 else cg[...] + term

    def image(tile):
        rows = pl.ds(tile * IMG, IMG)
        x_v[rows, :] = lax.dot_general(dq_v[rows, :], qw_v[...], NT, preferred_element_type=F32).astype(BF16)
        stores.append(keep(x_v.at[rows], image_out.at[rows], store_sem.at[CHUNKS + tile]))

    attend(0)
    attend(1)
    attend(2)
    attend(3)
    add_up(0)
    image(0)
    add_up(1)
    add_up(2)
    image(1)
    spread(0)
    add_up(3)
    spread(1)
    image(2)
    finish(0)
    spread(2)
    finish(1)
    spread(3)
    finish(2)
    image(3)
    finish(3)
    for k in (2, 1, 3):
        to = turn(y, k, NY)
        send(cg.at[to], caption_out.at[:, columns(y)], sent.at[7], o_r, at(to, x, z, c))
    stores.append(keep(cg.at[y], caption_out.at[:, columns(y)], store_sem.at[CHUNKS + SAMP]))
    take(sent.at[0], caps.at[pl.ds(0, NY - 1)])
    take(sent.at[1], rs)
    take(sent.at[2], sel.at[:, pl.ds(0, PROMPTS - 1)])
    take(sent.at[3], sel.at[:, seven])
    take(sent.at[4], sel.at[:, seven])
    take(sent.at[5], r1)
    take(sent.at[6], sel.at[0, seven])
    for store in stores:
        store.wait()
    take(o_r, cg.at[pl.ds(0, NY - 1)])
    take(sent.at[7], cg.at[pl.ds(0, NY - 1)])


def shards(captions, kv_weight, image_tokens, q_weight, context_grad, sample_prompt, caption_len):
    any_space = pl.BlockSpec(memory_space=pl.ANY)
    smem = pl.BlockSpec(memory_space=pltpu.SMEM)
    dma = pltpu.SemaphoreType.DMA
    rows = SAMP * IMG

    context, image_grad, caption_grad = pl.pallas_call(
        kernel,
        out_shape=(
            jax.ShapeDtypeStruct((rows, INNER), BF16),
            jax.ShapeDtypeStruct((rows, CIMG), BF16),
            jax.ShapeDtypeStruct((TOK, WIDE), F32),
        ),
        in_specs=[smem, smem] + [any_space] * 5,
        out_specs=(any_space,) * 3,
        scratch_shapes=[
            pltpu.VMEM((DEPTH, 2 * INNER), BF16),
            pltpu.VMEM((rows, CIMG), BF16),
            pltpu.VMEM((CIMG, INNER), BF16),
            pltpu.VMEM((rows, INNER), BF16),
            pltpu.VMEM((rows, INNER), BF16),
            pltpu.VMEM((rows, INNER), BF16),
            pltpu.VMEM((rows, INNER), BF16),
            pltpu.VMEM((NY, TOK, DEPTH), BF16),
            pltpu.VMEM((CHUNKS, NY, TOK, 2 * CW), F32),
            pltpu.VMEM((CHUNKS, NY - 1, TOK, 2 * CW), F32),
            pltpu.VMEM((CHUNKS, 2, TOK, CW), BF16),
            pltpu.VMEM((CHUNKS, NY * NC * SAMP, TOK, CW), BF16),
            pltpu.VMEM((CHUNKS, 2, SAMP, NY, TOK, CW), BF16),
            pltpu.VMEM((CHUNKS, 2, SAMP, NY, TOK, CW), BF16),
            pltpu.VMEM((CHUNKS, NY, NC, SAMP, TOK, CW), BF16),
            pltpu.VMEM((PROMPTS * TOK, NY * NC * SAMP * TOK), BF16),
            pltpu.VMEM((CHUNKS, NX, NZ, NC, TOK, CW), F32),
            pltpu.VMEM((CHUNKS, NX, NZ, NC, TOK, CW), BF16),
            pltpu.VMEM((CHUNKS, NX * NZ - 1, NC, TOK, CW), BF16),
            pltpu.VMEM((CHUNKS, NC, TOK, CW), BF16),
            pltpu.VMEM((CHUNKS, 2, NY, TOK, CW), BF16),
            pltpu.VMEM((NY, TOK, DEPTH), F32),
            dma((5,)),
            dma((8,)),
            dma,
            dma((CHUNKS,)),
            dma((CHUNKS,)),
            dma((CHUNKS,)),
            dma((CHUNKS,)),
            dma((CHUNKS,)),
            dma((CHUNKS,)),
            dma,
            dma((CHUNKS + SAMP + 1,)),
        ] + [pltpu.VMEM((PROMPTS, TOK, CW), BF16) for _ in range(CHUNKS)],
        compiler_params=pltpu.CompilerParams(
            collective_id=0, has_side_effects=True, vmem_limit_bytes=VMEM_LIMIT
        ),
    )(
        sample_prompt,
        caption_len,
        captions.reshape(TOK, WIDE),
        kv_weight,
        image_tokens.reshape(rows, CIMG),
        q_weight,
        context_grad.reshape(rows, INNER),
    )
    return (
        context.reshape(SAMP, IMG, INNER),
        image_grad.reshape(SAMP, IMG, CIMG),
        caption_grad.reshape(1, TOK, WIDE),
    )


def solution(mesh):
    placed = (
        P("dev", "grp", None),
        P("grp", None),
        P(("grp", "dev"), None, None),
        P(),
        P(("grp", "dev"), None, None),
        P(),
        P(),
    )
    return jax.shard_map(
        shards,
        mesh=mesh,
        in_specs=placed,
        out_specs=(
            P(("grp", "dev"), None, None),
            P(("grp", "dev"), None, None),
            P("dev", "grp", None),
        ),
        check_vma=False,
    )
```

```python
import math

import jax
import jax.numpy as jnp
from jax import lax
from jax.experimental import pallas as pl
from jax.experimental.pallas import tpu as pltpu
from jax.sharding import PartitionSpec as P

HEADS = 8
HD = 128
NEG_FILL = -1e30
MESH = pl.DeviceIdType.MESH
BF16 = jnp.bfloat16
F32 = jnp.float32
VMEM_LIMIT = 44 * 1024 * 1024

NY, NX, NZ, NC = 4, 4, 4, 2
SAMP = 4
TOK = 16
INNER = 1024
WIDE = 4096
DEPTH = 1024
IMG = 256
CIMG = 2048
PROMPTS = 32
CHUNKS = 4
CW = INNER // CHUNKS
LINE = [(k, j) for k in (2, 1, 3, 0) for j in (1, 0)]
NT = (((1,), (1,)), ((), ()))
TN = (((0,), (0,)), ((), ()))


def place():
    grp = lax.axis_index("grp")
    dev = lax.axis_index("dev")
    return grp, lax.div(dev, 8), lax.rem(lax.div(dev, 2), 4), lax.rem(dev, 2)


def at(grp, x, z, core):
    return {"grp": grp, "dev": (x * NZ + z) * NC + core}


def turn(index, step, size):
    return lax.rem(index + step, size)


def greet():
    y, x, z, c = place()
    barrier = pltpu.get_barrier_semaphore()
    peers = [at(turn(y, k, NY), x, z, c) for k in range(1, NY)]
    peers += [at(y, turn(x, k, NX), z, c) for k in range(1, NX)]
    peers += [at(y, x, turn(z, k, NZ), c) for k in range(1, NZ)]
    peers += [at(y, x, z, 1 - c)]
    for peer in peers:
        pl.semaphore_signal(barrier, inc=1, device_id=peer, device_id_type=MESH)
    pl.semaphore_wait(barrier, len(peers))


def pass_on(line_sem):
    y, x, z, c = place()
    for k in range(1, NX):
        pl.semaphore_signal(line_sem, inc=1, device_id=at(y, turn(x, k, NX), z, c), device_id_type=MESH)


def hear(line_sem, pair_sem):
    y, x, z, c = place()
    pl.semaphore_wait(line_sem, NX - 1)
    pl.semaphore_signal(pair_sem, inc=1, device_id=at(y, x, z, 1 - c), device_id_type=MESH)
    pl.semaphore_wait(pair_sem, 1)


def send(src, dst, send_sem, recv_sem, peer):
    pltpu.make_async_remote_copy(
        src_ref=src, dst_ref=dst, send_sem=send_sem, recv_sem=recv_sem, device_id=peer, device_id_type=MESH
    ).start()


def take(sem, like):
    pltpu.make_async_copy(like, like, sem).wait()


def kernel(
    prompt_hbm, len_hbm, cap_hbm, w_hbm, x_hbm, qw_hbm, g_hbm, context_out, image_out, caption_out, *scratch
):
    (
        prompt_ref, len_ref, w_v, x_v, qw_v, q_v, g_v, dq_v, cap_v, caps, part, rs, kvb, sel, skv, dkv, arr, match,
        sums, rsb, r1, kvg, full, cg,
        load_sem, sent, cap_r, rs_r, ag_r, sel_r, grad_r, r1_r, f_r, o_r, line_sem, pair_sem,
    ) = scratch[:-CHUNKS]
    gath = scratch[-CHUNKS:]
    y, x, z, c = place()

    def columns(index):
        return pl.ds(pl.multiple_of(index * DEPTH, DEPTH), DEPTH)

    def keep(src, dst, sem):
        copy = pltpu.make_async_copy(src, dst, sem)
        copy.start()
        return copy

    load_cap = keep(cap_hbm, cap_v, load_sem.at[0])
    load_prompt = keep(prompt_hbm, prompt_ref, load_sem.at[5])
    load_len = keep(len_hbm, len_ref, load_sem.at[6])
    load_w = keep(w_hbm, w_v, load_sem.at[1])
    load_cap.wait()
    greet()

    for k in (2, 1, 3):
        to = turn(y, k, NY)
        send(cap_v.at[:, columns(to)], caps.at[y], sent.at[0], cap_r, at(to, x, z, c))
    caps[y] = cap_v[:, columns(y)]
    pass_on(line_sem)
    load_w.wait()
    load_qw = keep(qw_hbm, qw_v, load_sem.at[3])
    load_x = keep(x_hbm, x_v, load_sem.at[2])
    take(cap_r, caps.at[pl.ds(0, NY - 1)])
    hear(line_sem, pair_sem)

    def project(tile):
        rows = pl.ds(tile * IMG, IMG)
        q_v[rows, :] = jnp.dot(x_v[rows, :], qw_v[...], preferred_element_type=F32).astype(BF16)

    def partial(q):
        lhs = caps[...].reshape(NY * TOK, DEPTH)
        for half in range(2):
            part[q, :, :, pl.ds(half * CW, CW)] = jnp.dot(
                lhs, w_v[:, pl.ds(half * INNER + q * CW, CW)], preferred_element_type=F32
            ).reshape(NY, TOK, CW)
        for k in (2, 1, 3):
            to = turn(y, k, NY)
            send(part.at[q, to], rs.at[q, k - 1], sent.at[1], rs_r.at[q], at(to, x, z, c))

    me = (x * NZ + z) * NC + c

    def gather(q):
        take(rs_r.at[q], rs.at[q])
        whole = (part[q, y] + rs[q, 0] + rs[q, 1] + rs[q, 2]).astype(BF16)
        kvb[q, 0] = whole[:, :CW]
        kvb[q, 1] = whole[:, CW:]
        for i in (2, 1, 3, 0):
            for j in (2, 1, 3, 0):
                for k in range(NC):
                    if i or j or k:
                        to_c = turn(c, k, NC)
                        send(
                            kvb.at[q, to_c], gath[q].at[me], sent.at[2], ag_r.at[q],
                            at(y, turn(x, i, NX), turn(z, j, NZ), to_c),
                        )
        gath[q][me] = kvb[q, c]

    def select(q):
        take(ag_r.at[q], gath[q].at[pl.ds(0, PROMPTS - 1)])
        for slot, (k, j) in enumerate(LINE):
            to_y, to_c = turn(y, k, NY), turn(c, j, NC)
            start = (to_y * (NX * NZ * NC) + (x * NZ + z) * NC + to_c) * SAMP
            for i in range(SAMP):
                block = gath[q][prompt_ref[start + i]]
                if k or j:
                    sel[q, slot * SAMP + i] = block
                else:
                    skv[q, c, i, y] = block
            if k or j:
                send(sel.at[q, pl.ds(slot * SAMP, SAMP)], skv.at[q, c, :, y], sent.at[3], sel_r.at[q], at(to_y, x, z, to_c))

    count = NY * NC * SAMP * TOK

    def one_hot():
        lanes = lax.broadcasted_iota(jnp.int32, (1, count), 1)
        owner = jnp.zeros((1, count), jnp.int32)
        for yy in range(NY):
            for cc in range(NC):
                for i in range(SAMP):
                    spot = (yy * NC + cc) * SAMP + i
                    p = prompt_ref[(yy * (NX * NZ * NC) + (x * NZ + z) * NC + cc) * SAMP + i]
                    owner = jnp.where(lanes // TOK == spot, p, owner)
        wanted = owner * TOK + lanes % TOK
        ids = lax.broadcasted_iota(jnp.int32, (PROMPTS * TOK, count), 0)
        match[...] = jnp.where(ids == wanted, 1.0, 0.0).astype(BF16)

    partial(0)
    load_prompt.wait()
    load_len.wait()
    load_qw.wait()
    load_x.wait()
    load_g = keep(g_hbm, g_v, load_sem.at[4])
    project(0)
    partial(1)
    project(1)
    gather(0)
    partial(2)
    partial(3)
    gather(1)
    project(2)
    gather(2)
    select(0)
    project(3)
    gather(3)
    select(1)
    select(2)
    select(3)
    one_hot()
    load_g.wait()

    scale = 1.0 / math.sqrt(HD)
    base = (y * (NX * NZ * NC) + (x * NZ + z) * NC + c) * SAMP
    tokens = NY * TOK

    def attention(q, s):
        rows = pl.ds(pl.multiple_of(s * IMG, IMG), IMG)
        cols = pl.ds(q * CW, CW)
        length = len_ref[prompt_ref[base + s]]
        live = lax.broadcasted_iota(jnp.int32, (2, tokens, IMG), 1) < length
        lead = lax.broadcasted_iota(jnp.int32, (tokens, CW), 1) < HD
        queries = q_v[rows, cols]
        grads = g_v[rows, cols]
        key = skv[q, 0, s].reshape(tokens, CW)
        value = skv[q, 1, s].reshape(tokens, CW)
        zero = jnp.zeros_like(key)
        key2 = jnp.concatenate([jnp.where(lead, key, zero), jnp.where(lead, zero, key)], axis=0)
        value2 = jnp.concatenate([jnp.where(lead, value, zero), jnp.where(lead, zero, value)], axis=0)
        scores = lax.dot_general(key2, queries, NT, preferred_element_type=F32) * scale
        scores = jnp.where(live, scores.reshape(2, tokens, IMG), NEG_FILL)
        expd = jnp.exp(scores - jnp.max(scores, axis=1, keepdims=True))
        soft = expd * (1.0 / jnp.sum(expd, axis=1, keepdims=True))
        soft_b = soft.astype(BF16).reshape(2 * tokens, IMG)
        d_soft = lax.dot_general(value2, grads, NT, preferred_element_type=F32).reshape(2, tokens, IMG)
        inner = jnp.sum(d_soft * soft, axis=1, keepdims=True)
        d_scores = (soft * (d_soft - inner) * scale).astype(BF16).reshape(2 * tokens, IMG)
        context_out[rows, cols] = lax.dot_general(soft_b, value2, TN, preferred_element_type=F32).astype(BF16)
        dq_v[rows, cols] = lax.dot_general(d_scores, key2, TN, preferred_element_type=F32).astype(BF16)
        d_key = jnp.dot(d_scores, queries, preferred_element_type=F32)
        d_value = jnp.dot(soft_b, grads, preferred_element_type=F32)
        dkv[q, 0, s] = jnp.where(lead, d_key[:tokens], d_key[tokens:]).astype(BF16).reshape(NY, TOK, CW)
        dkv[q, 1, s] = jnp.where(lead, d_value[:tokens], d_value[tokens:]).astype(BF16).reshape(NY, TOK, CW)

    seven = pl.ds(0, (NY * NC - 1) * SAMP)

    def attend(q):
        take(sel_r.at[q], sel.at[q, seven])

        def two(t, carry):
            attention(q, 2 * t)
            attention(q, 2 * t + 1)
            return carry

        lax.fori_loop(0, SAMP // 2, two, 0)
        for k, j in LINE[:-1]:
            to_y, to_c = turn(y, k, NY), turn(c, j, NC)
            send(dkv.at[q, to_c, :, to_y], arr.at[q, y, c], sent.at[4], grad_r.at[q], at(to_y, x, z, to_c))
        arr[q, y, c] = dkv[q, c, :, y]

    def add_up(q):
        take(grad_r.at[q], sel.at[q, seven])
        total = jnp.dot(match[...], arr[q].reshape(count, CW), preferred_element_type=F32)
        total = total.reshape(NX, NZ, NC, TOK, CW)
        sums[q] = total
        rsb[q] = total.astype(BF16)
        for i in (2, 1, 3, 0):
            for j in (2, 1, 3, 0):
                if i or j:
                    to_x, to_z = turn(x, i, NX), turn(z, j, NZ)
                    send(
                        rsb.at[q, to_x, to_z], r1.at[q, i * NZ + j - 1], sent.at[5], r1_r.at[q],
                        at(y, to_x, to_z, c),
                    )

    def spread(q):
        take(r1_r.at[q], r1.at[q])
        own = sums[q, x, z]
        for slot in range(NX * NZ - 1):
            own = own + r1[q, slot].astype(F32)
        kvg[q] = own.astype(BF16)
        for k, j in LINE[:-1]:
            to_y, to_c = turn(y, k, NY), turn(c, j, NC)
            send(kvg.at[q, to_c], full.at[q, c, y], sent.at[6], f_r.at[q], at(to_y, x, z, to_c))
        full[q, c, y] = kvg[q, c]

    def finish(q):
        take(f_r.at[q], gath[q].at[pl.ds(0, NY * NC - 1)])
        term = None
        for half in range(2):
            more = lax.dot_general(
                full[q, half].reshape(tokens, CW), w_v[:, pl.ds(half * INNER + q * CW, CW)], NT,
                preferred_element_type=F32,
            )
            term = more if term is None else term + more
        term = term.reshape(NY, TOK, DEPTH)
        cg[...] = term if q == 0 else cg[...] + term

    def image(tile):
        rows = pl.ds(tile * IMG, IMG)
        image_out[rows, :] = lax.dot_general(dq_v[rows, :], qw_v[...], NT, preferred_element_type=F32).astype(BF16)

    attend(0)
    attend(1)
    attend(2)
    attend(3)
    add_up(0)
    image(0)
    add_up(1)
    add_up(2)
    image(1)
    spread(0)
    add_up(3)
    spread(1)
    image(2)
    finish(0)
    spread(2)
    finish(1)
    spread(3)
    finish(2)
    image(3)
    finish(3)
    for k in (2, 1, 3):
        to = turn(y, k, NY)
        send(cg.at[to], caption_out.at[:, columns(y)], sent.at[7], o_r, at(to, x, z, c))
    caption_out[:, columns(y)] = cg[y]
    take(sent.at[0], caps.at[pl.ds(0, NY - 1)])
    take(sent.at[1], rs)
    take(sent.at[2], sel.at[:, pl.ds(0, PROMPTS - 1)])
    take(sent.at[3], sel.at[:, seven])
    take(sent.at[4], sel.at[:, seven])
    take(sent.at[5], r1)
    take(sent.at[6], sel.at[0, seven])
    take(o_r, cg.at[pl.ds(0, NY - 1)])
    take(sent.at[7], cg.at[pl.ds(0, NY - 1)])


def shards(captions, kv_weight, image_tokens, q_weight, context_grad, sample_prompt, caption_len):
    hbm = pl.BlockSpec(memory_space=pltpu.HBM)
    vmem = pl.BlockSpec(memory_space=pltpu.VMEM)
    dma = pltpu.SemaphoreType.DMA
    rows = SAMP * IMG

    context, image_grad, caption_grad = pl.pallas_call(
        kernel,
        out_shape=(
            pltpu.VMEM((rows, INNER), BF16),
            pltpu.VMEM((rows, CIMG), BF16),
            pltpu.VMEM((TOK, WIDE), F32),
        ),
        in_specs=[hbm] * 7,
        out_specs=(vmem,) * 3,
        scratch_shapes=[
            pltpu.SMEM(sample_prompt.shape, jnp.int32),
            pltpu.SMEM(caption_len.shape, jnp.int32),
            pltpu.VMEM((DEPTH, 2 * INNER), BF16),
            pltpu.VMEM((rows, CIMG), BF16),
            pltpu.VMEM((CIMG, INNER), BF16),
            pltpu.VMEM((rows, INNER), BF16),
            pltpu.VMEM((rows, INNER), BF16),
            pltpu.VMEM((rows, INNER), BF16),
            pltpu.VMEM((TOK, WIDE), BF16),
            pltpu.VMEM((NY, TOK, DEPTH), BF16),
            pltpu.VMEM((CHUNKS, NY, TOK, 2 * CW), F32),
            pltpu.VMEM((CHUNKS, NY - 1, TOK, 2 * CW), F32),
            pltpu.VMEM((CHUNKS, 2, TOK, CW), BF16),
            pltpu.VMEM((CHUNKS, NY * NC * SAMP, TOK, CW), BF16),
            pltpu.VMEM((CHUNKS, 2, SAMP, NY, TOK, CW), BF16),
            pltpu.VMEM((CHUNKS, 2, SAMP, NY, TOK, CW), BF16),
            pltpu.VMEM((CHUNKS, NY, NC, SAMP, TOK, CW), BF16),
            pltpu.VMEM((PROMPTS * TOK, NY * NC * SAMP * TOK), BF16),
            pltpu.VMEM((CHUNKS, NX, NZ, NC, TOK, CW), F32),
            pltpu.VMEM((CHUNKS, NX, NZ, NC, TOK, CW), BF16),
            pltpu.VMEM((CHUNKS, NX * NZ - 1, NC, TOK, CW), BF16),
            pltpu.VMEM((CHUNKS, NC, TOK, CW), BF16),
            pltpu.VMEM((CHUNKS, 2, NY, TOK, CW), BF16),
            pltpu.VMEM((NY, TOK, DEPTH), F32),
            dma((7,)),
            dma((8,)),
            dma,
            dma((CHUNKS,)),
            dma((CHUNKS,)),
            dma((CHUNKS,)),
            dma((CHUNKS,)),
            dma((CHUNKS,)),
            dma((CHUNKS,)),
            dma,
            pltpu.SemaphoreType.REGULAR,
            pltpu.SemaphoreType.REGULAR,
        ] + [pltpu.VMEM((PROMPTS, TOK, CW), BF16) for _ in range(CHUNKS)],
        compiler_params=pltpu.CompilerParams(
            collective_id=0, has_side_effects=True, vmem_limit_bytes=VMEM_LIMIT
        ),
    )(*[
        pltpu.with_memory_space_constraint(operand, pltpu.HBM)
        for operand in (
            sample_prompt,
            caption_len,
            captions.reshape(TOK, WIDE),
            kv_weight,
            image_tokens.reshape(rows, CIMG),
            q_weight,
            context_grad.reshape(rows, INNER),
        )
    ])
    return (
        context.reshape(SAMP, IMG, INNER),
        image_grad.reshape(SAMP, IMG, CIMG),
        caption_grad.reshape(1, TOK, WIDE),
    )


def solution(mesh):
    placed = (
        P("dev", "grp", None),
        P("grp", None),
        P(("grp", "dev"), None, None),
        P(),
        P(("grp", "dev"), None, None),
        P(),
        P(),
    )
    return jax.shard_map(
        shards,
        mesh=mesh,
        in_specs=placed,
        out_specs=(
            P(("grp", "dev"), None, None),
            P(("grp", "dev"), None, None),
            P("dev", "grp", None),
        ),
        check_vma=False,
    )
```

```python
import math

import jax
import jax.numpy as jnp
from jax import lax
from jax.experimental import pallas as pl
from jax.experimental.pallas import tpu as pltpu
from jax.sharding import PartitionSpec as P

HEADS = 8
HD = 128
NEG_FILL = -1e30
MESH = pl.DeviceIdType.MESH
BF16 = jnp.bfloat16
F32 = jnp.float32
VMEM_LIMIT = 44 * 1024 * 1024

NY, NX, NZ, NC = 4, 4, 4, 2
SAMP = 4
TOK = 16
INNER = 1024
WIDE = 4096
DEPTH = 1024
IMG = 256
CIMG = 2048
PROMPTS = 32
CHUNKS = 4
CW = INNER // CHUNKS
LINE = [(k, j) for k in (2, 1, 3, 0) for j in (1, 0)]
NT = (((1,), (1,)), ((), ()))
TN = (((0,), (0,)), ((), ()))


def place():
    grp = lax.axis_index("grp")
    dev = lax.axis_index("dev")
    return grp, lax.div(dev, 8), lax.rem(lax.div(dev, 2), 4), lax.rem(dev, 2)


def at(grp, x, z, core):
    return {"grp": grp, "dev": (x * NZ + z) * NC + core}


def turn(index, step, size):
    return lax.rem(index + step, size)


def greet():
    y, x, z, c = place()
    barrier = pltpu.get_barrier_semaphore()
    peers = [at(turn(y, k, NY), x, z, c) for k in range(1, NY)]
    peers += [at(y, turn(x, k, NX), z, c) for k in range(1, NX)]
    peers += [at(y, x, turn(z, k, NZ), c) for k in range(1, NZ)]
    peers += [at(y, x, z, 1 - c)]
    for peer in peers:
        pl.semaphore_signal(barrier, inc=1, device_id=peer, device_id_type=MESH)
    pl.semaphore_wait(barrier, len(peers))


def pass_on(line_sem):
    y, x, z, c = place()
    for k in range(1, NX):
        pl.semaphore_signal(line_sem, inc=1, device_id=at(y, turn(x, k, NX), z, c), device_id_type=MESH)


def hear(line_sem, pair_sem):
    y, x, z, c = place()
    pl.semaphore_wait(line_sem, NX - 1)
    pl.semaphore_signal(pair_sem, inc=1, device_id=at(y, x, z, 1 - c), device_id_type=MESH)
    pl.semaphore_wait(pair_sem, 1)


def send(src, dst, send_sem, recv_sem, peer):
    pltpu.make_async_remote_copy(
        src_ref=src, dst_ref=dst, send_sem=send_sem, recv_sem=recv_sem, device_id=peer, device_id_type=MESH
    ).start()


def take(sem, like):
    pltpu.make_async_copy(like, like, sem).wait()


def kernel(
    prompt_hbm, len_hbm, cap_hbm, w_hbm, x_hbm, qw_hbm, g_hbm, context_out, image_out, caption_out, *scratch
):
    (
        prompt_ref, len_ref, w_v, x_v, qw_v, q_v, g_v, dq_v, cap_v, caps, part, rs, kvb, sel, skv, dkv, arr, match,
        sums, rsb, r1, kvg, full, cg, late, late_b, early, late_in,
        load_sem, sent, cap_r, rs_r, ag_r, sel_r, grad_r, r1_r, f_r, o_r, early_r, line_sem, pair_sem,
    ) = scratch[:-CHUNKS]
    gath = scratch[-CHUNKS:]
    y, x, z, c = place()

    def columns(index):
        return pl.ds(pl.multiple_of(index * DEPTH, DEPTH), DEPTH)

    def keep(src, dst, sem):
        copy = pltpu.make_async_copy(src, dst, sem)
        copy.start()
        return copy

    load_cap = keep(cap_hbm, cap_v, load_sem.at[0])
    load_prompt = keep(prompt_hbm, prompt_ref, load_sem.at[5])
    load_len = keep(len_hbm, len_ref, load_sem.at[6])
    load_w = keep(w_hbm, w_v, load_sem.at[1])
    load_cap.wait()
    greet()

    for k in (2, 1, 3):
        to = turn(y, k, NY)
        send(cap_v.at[:, columns(to)], caps.at[y], sent.at[0], cap_r, at(to, x, z, c))
    caps[y] = cap_v[:, columns(y)]
    pass_on(line_sem)
    load_w.wait()
    load_qw = keep(qw_hbm, qw_v, load_sem.at[3])
    load_x = keep(x_hbm, x_v, load_sem.at[2])
    take(cap_r, caps.at[pl.ds(0, NY - 1)])
    hear(line_sem, pair_sem)

    def project(tile):
        rows = pl.ds(tile * IMG, IMG)
        q_v[rows, :] = jnp.dot(x_v[rows, :], qw_v[...], preferred_element_type=F32).astype(BF16)

    def partial(q):
        lhs = caps[...].reshape(NY * TOK, DEPTH)
        for half in range(2):
            part[q, :, :, pl.ds(half * CW, CW)] = jnp.dot(
                lhs, w_v[:, pl.ds(half * INNER + q * CW, CW)], preferred_element_type=F32
            ).reshape(NY, TOK, CW)
        for k in (2, 1, 3):
            to = turn(y, k, NY)
            send(part.at[q, to], rs.at[q, k - 1], sent.at[1], rs_r.at[q], at(to, x, z, c))

    me = (x * NZ + z) * NC + c

    def gather(q):
        take(rs_r.at[q], rs.at[q])
        whole = (part[q, y] + rs[q, 0] + rs[q, 1] + rs[q, 2]).astype(BF16)
        kvb[q, 0] = whole[:, :CW]
        kvb[q, 1] = whole[:, CW:]
        for i in (2, 1, 3, 0):
            for j in (2, 1, 3, 0):
                for k in range(NC):
                    if i or j or k:
                        to_c = turn(c, k, NC)
                        send(
                            kvb.at[q, to_c], gath[q].at[me], sent.at[2], ag_r.at[q],
                            at(y, turn(x, i, NX), turn(z, j, NZ), to_c),
                        )
        gath[q][me] = kvb[q, c]

    def select(q):
        take(ag_r.at[q], gath[q].at[pl.ds(0, PROMPTS - 1)])
        for slot, (k, j) in enumerate(LINE):
            to_y, to_c = turn(y, k, NY), turn(c, j, NC)
            start = (to_y * (NX * NZ * NC) + (x * NZ + z) * NC + to_c) * SAMP
            for i in range(SAMP):
                block = gath[q][prompt_ref[start + i]]
                if k or j:
                    sel[q, slot * SAMP + i] = block
                else:
                    skv[q, c, i, y] = block
            if k or j:
                send(sel.at[q, pl.ds(slot * SAMP, SAMP)], skv.at[q, c, :, y], sent.at[3], sel_r.at[q], at(to_y, x, z, to_c))

    count = NY * NC * SAMP * TOK

    def one_hot():
        lanes = lax.broadcasted_iota(jnp.int32, (1, count), 1)
        owner = jnp.zeros((1, count), jnp.int32)
        for yy in range(NY):
            for cc in range(NC):
                for i in range(SAMP):
                    spot = (yy * NC + cc) * SAMP + i
                    p = prompt_ref[(yy * (NX * NZ * NC) + (x * NZ + z) * NC + cc) * SAMP + i]
                    owner = jnp.where(lanes // TOK == spot, p, owner)
        wanted = owner * TOK + lanes % TOK
        ids = lax.broadcasted_iota(jnp.int32, (PROMPTS * TOK, count), 0)
        match[...] = jnp.where(ids == wanted, 1.0, 0.0).astype(BF16)

    partial(0)
    load_prompt.wait()
    load_len.wait()
    load_qw.wait()
    load_x.wait()
    load_g = keep(g_hbm, g_v, load_sem.at[4])
    project(0)
    partial(1)
    project(1)
    gather(0)
    partial(2)
    partial(3)
    gather(1)
    project(2)
    gather(2)
    select(0)
    project(3)
    gather(3)
    select(1)
    select(2)
    select(3)
    one_hot()
    load_g.wait()

    scale = 1.0 / math.sqrt(HD)
    base = (y * (NX * NZ * NC) + (x * NZ + z) * NC + c) * SAMP
    tokens = NY * TOK

    def attention(q, s):
        rows = pl.ds(pl.multiple_of(s * IMG, IMG), IMG)
        cols = pl.ds(q * CW, CW)
        length = len_ref[prompt_ref[base + s]]
        live = lax.broadcasted_iota(jnp.int32, (2, tokens, IMG), 1) < length
        lead = lax.broadcasted_iota(jnp.int32, (tokens, CW), 1) < HD
        queries = q_v[rows, cols]
        grads = g_v[rows, cols]
        key = skv[q, 0, s].reshape(tokens, CW)
        value = skv[q, 1, s].reshape(tokens, CW)
        zero = jnp.zeros_like(key)
        key2 = jnp.concatenate([jnp.where(lead, key, zero), jnp.where(lead, zero, key)], axis=0)
        value2 = jnp.concatenate([jnp.where(lead, value, zero), jnp.where(lead, zero, value)], axis=0)
        scores = lax.dot_general(key2, queries, NT, preferred_element_type=F32) * scale
        scores = jnp.where(live, scores.reshape(2, tokens, IMG), NEG_FILL)
        expd = jnp.exp(scores - jnp.max(scores, axis=1, keepdims=True))
        soft = expd * (1.0 / jnp.sum(expd, axis=1, keepdims=True))
        soft_b = soft.astype(BF16).reshape(2 * tokens, IMG)
        d_soft = lax.dot_general(value2, grads, NT, preferred_element_type=F32).reshape(2, tokens, IMG)
        inner = jnp.sum(d_soft * soft, axis=1, keepdims=True)
        d_scores = (soft * (d_soft - inner) * scale).astype(BF16).reshape(2 * tokens, IMG)
        context_out[rows, cols] = lax.dot_general(soft_b, value2, TN, preferred_element_type=F32).astype(BF16)
        dq_v[rows, cols] = lax.dot_general(d_scores, key2, TN, preferred_element_type=F32).astype(BF16)
        d_key = jnp.dot(d_scores, queries, preferred_element_type=F32)
        d_value = jnp.dot(soft_b, grads, preferred_element_type=F32)
        dkv[q, 0, s] = jnp.where(lead, d_key[:tokens], d_key[tokens:]).astype(BF16).reshape(NY, TOK, CW)
        dkv[q, 1, s] = jnp.where(lead, d_value[:tokens], d_value[tokens:]).astype(BF16).reshape(NY, TOK, CW)

    seven = pl.ds(0, (NY * NC - 1) * SAMP)

    def attend(q):
        take(sel_r.at[q], sel.at[q, seven])

        def two(t, carry):
            attention(q, 2 * t)
            attention(q, 2 * t + 1)
            return carry

        lax.fori_loop(0, SAMP // 2, two, 0)
        for k, j in LINE[:-1]:
            to_y, to_c = turn(y, k, NY), turn(c, j, NC)
            send(dkv.at[q, to_c, :, to_y], arr.at[q, y, c], sent.at[4], grad_r.at[q], at(to_y, x, z, to_c))
        arr[q, y, c] = dkv[q, c, :, y]

    def add_up(q):
        take(grad_r.at[q], sel.at[q, seven])
        total = jnp.dot(match[...], arr[q].reshape(count, CW), preferred_element_type=F32)
        total = total.reshape(NX, NZ, NC, TOK, CW)
        sums[q] = total
        rsb[q] = total.astype(BF16)
        for i in (2, 1, 3, 0):
            for j in (2, 1, 3, 0):
                if i or j:
                    to_x, to_z = turn(x, i, NX), turn(z, j, NZ)
                    send(
                        rsb.at[q, to_x, to_z], r1.at[q, i * NZ + j - 1], sent.at[5], r1_r.at[q],
                        at(y, to_x, to_z, c),
                    )

    def spread(q):
        take(r1_r.at[q], r1.at[q])
        own = sums[q, x, z]
        for slot in range(NX * NZ - 1):
            own = own + r1[q, slot].astype(F32)
        kvg[q] = own.astype(BF16)
        for k, j in LINE[:-1]:
            to_y, to_c = turn(y, k, NY), turn(c, j, NC)
            send(kvg.at[q, to_c], full.at[q, c, y], sent.at[6], f_r.at[q], at(to_y, x, z, to_c))
        full[q, c, y] = kvg[q, c]

    def finish(q):
        take(f_r.at[q], gath[q].at[pl.ds(0, NY * NC - 1)])
        term = None
        for half in range(2):
            more = lax.dot_general(
                full[q, half].reshape(tokens, CW), w_v[:, pl.ds(half * INNER + q * CW, CW)], NT,
                preferred_element_type=F32,
            )
            term = more if term is None else term + more
        term = term.reshape(NY, TOK, DEPTH)
        held = cg if q < CHUNKS // 2 else late
        held[...] = term if q % (CHUNKS // 2) == 0 else held[...] + term

    def image(tile):
        rows = pl.ds(tile * IMG, IMG)
        image_out[rows, :] = lax.dot_general(dq_v[rows, :], qw_v[...], NT, preferred_element_type=F32).astype(BF16)

    attend(0)
    attend(1)
    attend(2)
    attend(3)
    add_up(0)
    image(0)
    add_up(1)
    add_up(2)
    image(1)
    spread(0)
    add_up(3)
    spread(1)
    image(2)
    finish(0)
    spread(2)
    finish(1)
    for k in (2, 1, 3):
        to = turn(y, k, NY)
        send(cg.at[to], early.at[k - 1], sent.at[7], early_r, at(to, x, z, c))
    spread(3)
    finish(2)
    image(3)
    finish(3)
    late_b[...] = late[...].astype(BF16)
    for k in (2, 1, 3):
        to = turn(y, k, NY)
        send(late_b.at[to], late_in.at[k - 1], sent.at[8], o_r, at(to, x, z, c))
    caption_out[:, columns(y)] = cg[y] + late[y]
    take(sent.at[0], caps.at[pl.ds(0, NY - 1)])
    take(sent.at[1], rs)
    take(sent.at[2], sel.at[:, pl.ds(0, PROMPTS - 1)])
    take(sent.at[3], sel.at[:, seven])
    take(sent.at[4], sel.at[:, seven])
    take(sent.at[5], r1)
    take(sent.at[6], sel.at[0, seven])
    take(early_r, early)
    take(o_r, late_in)
    for k in range(1, NY):
        caption_out[:, columns(turn(y, NY - k, NY))] = early[k - 1] + late_in[k - 1].astype(F32)
    take(sent.at[7], early)
    take(sent.at[8], late_in)


def shards(captions, kv_weight, image_tokens, q_weight, context_grad, sample_prompt, caption_len):
    hbm = pl.BlockSpec(memory_space=pltpu.HBM)
    vmem = pl.BlockSpec(memory_space=pltpu.VMEM)
    dma = pltpu.SemaphoreType.DMA
    rows = SAMP * IMG

    context, image_grad, caption_grad = pl.pallas_call(
        kernel,
        out_shape=(
            pltpu.VMEM((rows, INNER), BF16),
            pltpu.VMEM((rows, CIMG), BF16),
            pltpu.VMEM((TOK, WIDE), F32),
        ),
        in_specs=[hbm] * 7,
        out_specs=(vmem,) * 3,
        scratch_shapes=[
            pltpu.SMEM(sample_prompt.shape, jnp.int32),
            pltpu.SMEM(caption_len.shape, jnp.int32),
            pltpu.VMEM((DEPTH, 2 * INNER), BF16),
            pltpu.VMEM((rows, CIMG), BF16),
            pltpu.VMEM((CIMG, INNER), BF16),
            pltpu.VMEM((rows, INNER), BF16),
            pltpu.VMEM((rows, INNER), BF16),
            pltpu.VMEM((rows, INNER), BF16),
            pltpu.VMEM((TOK, WIDE), BF16),
            pltpu.VMEM((NY, TOK, DEPTH), BF16),
            pltpu.VMEM((CHUNKS, NY, TOK, 2 * CW), F32),
            pltpu.VMEM((CHUNKS, NY - 1, TOK, 2 * CW), F32),
            pltpu.VMEM((CHUNKS, 2, TOK, CW), BF16),
            pltpu.VMEM((CHUNKS, NY * NC * SAMP, TOK, CW), BF16),
            pltpu.VMEM((CHUNKS, 2, SAMP, NY, TOK, CW), BF16),
            pltpu.VMEM((CHUNKS, 2, SAMP, NY, TOK, CW), BF16),
            pltpu.VMEM((CHUNKS, NY, NC, SAMP, TOK, CW), BF16),
            pltpu.VMEM((PROMPTS * TOK, NY * NC * SAMP * TOK), BF16),
            pltpu.VMEM((CHUNKS, NX, NZ, NC, TOK, CW), F32),
            pltpu.VMEM((CHUNKS, NX, NZ, NC, TOK, CW), BF16),
            pltpu.VMEM((CHUNKS, NX * NZ - 1, NC, TOK, CW), BF16),
            pltpu.VMEM((CHUNKS, NC, TOK, CW), BF16),
            pltpu.VMEM((CHUNKS, 2, NY, TOK, CW), BF16),
            pltpu.VMEM((NY, TOK, DEPTH), F32),
            pltpu.VMEM((NY, TOK, DEPTH), F32),
            pltpu.VMEM((NY, TOK, DEPTH), BF16),
            pltpu.VMEM((NY - 1, TOK, DEPTH), F32),
            pltpu.VMEM((NY - 1, TOK, DEPTH), BF16),
            dma((7,)),
            dma((9,)),
            dma,
            dma((CHUNKS,)),
            dma((CHUNKS,)),
            dma((CHUNKS,)),
            dma((CHUNKS,)),
            dma((CHUNKS,)),
            dma((CHUNKS,)),
            dma,
            dma,
            pltpu.SemaphoreType.REGULAR,
            pltpu.SemaphoreType.REGULAR,
        ] + [pltpu.VMEM((PROMPTS, TOK, CW), BF16) for _ in range(CHUNKS)],
        compiler_params=pltpu.CompilerParams(
            collective_id=0, has_side_effects=True, vmem_limit_bytes=VMEM_LIMIT
        ),
    )(*[
        pltpu.with_memory_space_constraint(operand, pltpu.HBM)
        for operand in (
            sample_prompt,
            caption_len,
            captions.reshape(TOK, WIDE),
            kv_weight,
            image_tokens.reshape(rows, CIMG),
            q_weight,
            context_grad.reshape(rows, INNER),
        )
    ])
    return (
        context.reshape(SAMP, IMG, INNER),
        image_grad.reshape(SAMP, IMG, CIMG),
        caption_grad.reshape(1, TOK, WIDE),
    )


def solution(mesh):
    placed = (
        P("dev", "grp", None),
        P("grp", None),
        P(("grp", "dev"), None, None),
        P(),
        P(("grp", "dev"), None, None),
        P(),
        P(),
    )
    return jax.shard_map(
        shards,
        mesh=mesh,
        in_specs=placed,
        out_specs=(
            P(("grp", "dev"), None, None),
            P(("grp", "dev"), None, None),
            P("dev", "grp", None),
        ),
        check_vma=False,
    )
```

```python
import math

import jax
import jax.numpy as jnp
from jax import lax
from jax.experimental import pallas as pl
from jax.experimental.pallas import tpu as pltpu
from jax.sharding import PartitionSpec as P

HEADS = 8
HD = 128
NEG_FILL = -1e30
MESH = pl.DeviceIdType.MESH
BF16 = jnp.bfloat16
F32 = jnp.float32
VMEM_LIMIT = 44 * 1024 * 1024

NY, NX, NZ, NC = 4, 4, 4, 2
SAMP = 4
TOK = 16
INNER = 1024
WIDE = 4096
DEPTH = 1024
IMG = 256
CIMG = 2048
PROMPTS = 32
CHUNKS = 4
CW = INNER // CHUNKS
LINE = [(k, j) for k in (2, 1, 3, 0) for j in (1, 0)]
NT = (((1,), (1,)), ((), ()))
TN = (((0,), (0,)), ((), ()))


def place():
    grp = lax.axis_index("grp")
    dev = lax.axis_index("dev")
    return grp, lax.div(dev, 8), lax.rem(lax.div(dev, 2), 4), lax.rem(dev, 2)


def at(grp, x, z, core):
    return {"grp": grp, "dev": (x * NZ + z) * NC + core}


def turn(index, step, size):
    return lax.rem(index + step, size)


def greet():
    y, x, z, c = place()
    barrier = pltpu.get_barrier_semaphore()
    peers = [at(turn(y, k, NY), x, z, c) for k in range(1, NY)]
    peers += [at(y, turn(x, k, NX), z, c) for k in range(1, NX)]
    peers += [at(y, x, turn(z, k, NZ), c) for k in range(1, NZ)]
    peers += [at(y, x, z, 1 - c)]
    for peer in peers:
        pl.semaphore_signal(barrier, inc=1, device_id=peer, device_id_type=MESH)
    pl.semaphore_wait(barrier, len(peers))


def pass_on(line_sem):
    y, x, z, c = place()
    for k in range(1, NX):
        pl.semaphore_signal(line_sem, inc=1, device_id=at(y, turn(x, k, NX), z, c), device_id_type=MESH)


def hear(line_sem, pair_sem):
    y, x, z, c = place()
    pl.semaphore_wait(line_sem, NX - 1)
    pl.semaphore_signal(pair_sem, inc=1, device_id=at(y, x, z, 1 - c), device_id_type=MESH)
    pl.semaphore_wait(pair_sem, 1)


def send(src, dst, send_sem, recv_sem, peer):
    pltpu.make_async_remote_copy(
        src_ref=src, dst_ref=dst, send_sem=send_sem, recv_sem=recv_sem, device_id=peer, device_id_type=MESH
    ).start()


def take(sem, like):
    pltpu.make_async_copy(like, like, sem).wait()


def kernel(
    prompt_hbm, len_hbm, cap_hbm, w_hbm, x_hbm, qw_hbm, g_hbm, context_out, image_out, caption_out, *scratch
):
    (
        prompt_ref, len_ref, w_v, x_v, qw_v, q_v, g_v, dq_v, cap_v, caps, part, rs, kvb, sel, skv, dkv, arr, match,
        sums, rsb, r1, kvg, full, cg, late, late_b, early, late_in,
        load_sem, sent, cap_r, rs_r, ag_r, sel_r, grad_r, r1_r, f_r, o_r, early_r, line_sem, pair_sem,
    ) = scratch[:-CHUNKS]
    gath = scratch[-CHUNKS:]
    y, x, z, c = place()

    def columns(index):
        return pl.ds(pl.multiple_of(index * DEPTH, DEPTH), DEPTH)

    def keep(src, dst, sem):
        copy = pltpu.make_async_copy(src, dst, sem)
        copy.start()
        return copy

    load_cap = keep(cap_hbm, cap_v, load_sem.at[0])
    load_prompt = keep(prompt_hbm, prompt_ref, load_sem.at[5])
    load_len = keep(len_hbm, len_ref, load_sem.at[6])
    load_w = keep(w_hbm, w_v, load_sem.at[1])
    greet()
    load_cap.wait()

    for k in (2, 1, 3):
        to = turn(y, k, NY)
        send(cap_v.at[:, columns(to)], caps.at[y], sent.at[0], cap_r, at(to, x, z, c))
    caps[y] = cap_v[:, columns(y)]
    pass_on(line_sem)
    load_w.wait()
    load_qw = keep(qw_hbm, qw_v, load_sem.at[3])
    load_x = keep(x_hbm, x_v, load_sem.at[2])
    hear(line_sem, pair_sem)
    take(cap_r, caps.at[pl.ds(0, NY - 1)])

    def project(tile):
        rows = pl.ds(tile * IMG, IMG)
        q_v[rows, :] = jnp.dot(x_v[rows, :], qw_v[...], preferred_element_type=F32).astype(BF16)

    def partial(q):
        lhs = caps[...].reshape(NY * TOK, DEPTH)
        for half in range(2):
            part[q, :, :, pl.ds(half * CW, CW)] = jnp.dot(
                lhs, w_v[:, pl.ds(half * INNER + q * CW, CW)], preferred_element_type=F32
            ).reshape(NY, TOK, CW)
        for k in (2, 1, 3):
            to = turn(y, k, NY)
            send(part.at[q, to], rs.at[q, k - 1], sent.at[1], rs_r.at[q], at(to, x, z, c))

    me = (x * NZ + z) * NC + c

    def gather(q):
        take(rs_r.at[q], rs.at[q])
        whole = (part[q, y] + rs[q, 0] + rs[q, 1] + rs[q, 2]).astype(BF16)
        kvb[q, 0] = whole[:, :CW]
        kvb[q, 1] = whole[:, CW:]
        for i in (2, 1, 3, 0):
            for j in (2, 1, 3, 0):
                for k in range(NC):
                    if i or j or k:
                        to_c = turn(c, k, NC)
                        send(
                            kvb.at[q, to_c], gath[q].at[me], sent.at[2], ag_r.at[q],
                            at(y, turn(x, i, NX), turn(z, j, NZ), to_c),
                        )
        gath[q][me] = kvb[q, c]

    def select(q):
        take(ag_r.at[q], gath[q].at[pl.ds(0, PROMPTS - 1)])
        for slot, (k, j) in enumerate(LINE):
            to_y, to_c = turn(y, k, NY), turn(c, j, NC)
            start = (to_y * (NX * NZ * NC) + (x * NZ + z) * NC + to_c) * SAMP
            for i in range(SAMP):
                block = gath[q][prompt_ref[start + i]]
                if k or j:
                    sel[q, slot * SAMP + i] = block
                else:
                    skv[q, c, i, y] = block
            if k or j:
                send(sel.at[q, pl.ds(slot * SAMP, SAMP)], skv.at[q, c, :, y], sent.at[3], sel_r.at[q], at(to_y, x, z, to_c))

    count = NY * NC * SAMP * TOK

    def one_hot():
        lanes = lax.broadcasted_iota(jnp.int32, (1, count), 1)
        owner = jnp.zeros((1, count), jnp.int32)
        for yy in range(NY):
            for cc in range(NC):
                for i in range(SAMP):
                    spot = (yy * NC + cc) * SAMP + i
                    p = prompt_ref[(yy * (NX * NZ * NC) + (x * NZ + z) * NC + cc) * SAMP + i]
                    owner = jnp.where(lanes // TOK == spot, p, owner)
        wanted = owner * TOK + lanes % TOK
        ids = lax.broadcasted_iota(jnp.int32, (PROMPTS * TOK, count), 0)
        match[...] = jnp.where(ids == wanted, 1.0, 0.0).astype(BF16)

    partial(0)
    load_prompt.wait()
    load_len.wait()
    load_qw.wait()
    load_x.wait()
    load_g = keep(g_hbm, g_v, load_sem.at[4])
    project(0)
    partial(1)
    project(1)
    gather(0)
    partial(2)
    partial(3)
    gather(1)
    project(2)
    gather(2)
    select(0)
    project(3)
    gather(3)
    select(1)
    select(2)
    select(3)
    one_hot()
    load_g.wait()

    scale = 1.0 / math.sqrt(HD)
    base = (y * (NX * NZ * NC) + (x * NZ + z) * NC + c) * SAMP
    tokens = NY * TOK

    def attention(q, s):
        rows = pl.ds(pl.multiple_of(s * IMG, IMG), IMG)
        cols = pl.ds(q * CW, CW)
        length = len_ref[prompt_ref[base + s]]
        live = lax.broadcasted_iota(jnp.int32, (2, tokens, IMG), 1) < length
        lead = lax.broadcasted_iota(jnp.int32, (tokens, CW), 1) < HD
        queries = q_v[rows, cols]
        grads = g_v[rows, cols]
        key = skv[q, 0, s].reshape(tokens, CW)
        value = skv[q, 1, s].reshape(tokens, CW)
        zero = jnp.zeros_like(key)
        key2 = jnp.concatenate([jnp.where(lead, key, zero), jnp.where(lead, zero, key)], axis=0)
        value2 = jnp.concatenate([jnp.where(lead, value, zero), jnp.where(lead, zero, value)], axis=0)
        scores = lax.dot_general(key2, queries, NT, preferred_element_type=F32) * scale
        scores = jnp.where(live, scores.reshape(2, tokens, IMG), NEG_FILL)
        expd = jnp.exp(scores - jnp.max(scores, axis=1, keepdims=True))
        soft = expd * (1.0 / jnp.sum(expd, axis=1, keepdims=True))
        soft_b = soft.astype(BF16).reshape(2 * tokens, IMG)
        d_soft = lax.dot_general(value2, grads, NT, preferred_element_type=F32).reshape(2, tokens, IMG)
        inner = jnp.sum(d_soft * soft, axis=1, keepdims=True)
        d_scores = (soft * (d_soft - inner) * scale).astype(BF16).reshape(2 * tokens, IMG)
        context_out[rows, cols] = lax.dot_general(soft_b, value2, TN, preferred_element_type=F32).astype(BF16)
        dq_v[rows, cols] = lax.dot_general(d_scores, key2, TN, preferred_element_type=F32).astype(BF16)
        d_key = jnp.dot(d_scores, queries, preferred_element_type=F32)
        d_value = jnp.dot(soft_b, grads, preferred_element_type=F32)
        dkv[q, 0, s] = jnp.where(lead, d_key[:tokens], d_key[tokens:]).astype(BF16).reshape(NY, TOK, CW)
        dkv[q, 1, s] = jnp.where(lead, d_value[:tokens], d_value[tokens:]).astype(BF16).reshape(NY, TOK, CW)

    seven = pl.ds(0, (NY * NC - 1) * SAMP)

    def attend(q):
        take(sel_r.at[q], sel.at[q, seven])

        def two(t, carry):
            attention(q, 2 * t)
            attention(q, 2 * t + 1)
            return carry

        lax.fori_loop(0, SAMP // 2, two, 0)
        for k, j in LINE[:-1]:
            to_y, to_c = turn(y, k, NY), turn(c, j, NC)
            send(dkv.at[q, to_c, :, to_y], arr.at[q, y, c], sent.at[4], grad_r.at[q], at(to_y, x, z, to_c))
        arr[q, y, c] = dkv[q, c, :, y]

    def add_up(q):
        take(grad_r.at[q], sel.at[q, seven])
        total = jnp.dot(match[...], arr[q].reshape(count, CW), preferred_element_type=F32)
        total = total.reshape(NX, NZ, NC, TOK, CW)
        sums[q] = total
        rsb[q] = total.astype(BF16)
        for i in (2, 1, 3, 0):
            for j in (2, 1, 3, 0):
                if i or j:
                    to_x, to_z = turn(x, i, NX), turn(z, j, NZ)
                    send(
                        rsb.at[q, to_x, to_z], r1.at[q, i * NZ + j - 1], sent.at[5], r1_r.at[q],
                        at(y, to_x, to_z, c),
                    )

    def spread(q):
        take(r1_r.at[q], r1.at[q])
        own = sums[q, x, z]
        for slot in range(NX * NZ - 1):
            own = own + r1[q, slot].astype(F32)
        kvg[q] = own.astype(BF16)
        for k, j in LINE[:-1]:
            to_y, to_c = turn(y, k, NY), turn(c, j, NC)
            send(kvg.at[q, to_c], full.at[q, c, y], sent.at[6], f_r.at[q], at(to_y, x, z, to_c))
        full[q, c, y] = kvg[q, c]

    def finish(q):
        take(f_r.at[q], gath[q].at[pl.ds(0, NY * NC - 1)])
        term = None
        for half in range(2):
            more = lax.dot_general(
                full[q, half].reshape(tokens, CW), w_v[:, pl.ds(half * INNER + q * CW, CW)], NT,
                preferred_element_type=F32,
            )
            term = more if term is None else term + more
        term = term.reshape(NY, TOK, DEPTH)
        held = cg if q < CHUNKS // 2 else late
        held[...] = term if q % (CHUNKS // 2) == 0 else held[...] + term

    def image(tile):
        rows = pl.ds(tile * IMG, IMG)
        image_out[rows, :] = lax.dot_general(dq_v[rows, :], qw_v[...], NT, preferred_element_type=F32).astype(BF16)

    attend(0)
    attend(1)
    attend(2)
    attend(3)
    add_up(0)
    image(0)
    add_up(1)
    add_up(2)
    image(1)
    spread(0)
    add_up(3)
    spread(1)
    image(2)
    finish(0)
    spread(2)
    finish(1)
    for k in (2, 1, 3):
        to = turn(y, k, NY)
        send(cg.at[to], early.at[k - 1], sent.at[7], early_r, at(to, x, z, c))
    spread(3)
    finish(2)
    image(3)
    finish(3)
    late_b[...] = late[...].astype(BF16)
    for k in (2, 1, 3):
        to = turn(y, k, NY)
        send(late_b.at[to], late_in.at[k - 1], sent.at[8], o_r, at(to, x, z, c))
    caption_out[:, columns(y)] = cg[y] + late[y]
    take(sent.at[0], caps.at[pl.ds(0, NY - 1)])
    take(sent.at[1], rs)
    take(sent.at[2], sel.at[:, pl.ds(0, PROMPTS - 1)])
    take(sent.at[3], sel.at[:, seven])
    take(sent.at[4], sel.at[:, seven])
    take(sent.at[5], r1)
    take(sent.at[6], sel.at[0, seven])
    take(early_r, early)
    take(o_r, late_in)
    for k in range(1, NY):
        caption_out[:, columns(turn(y, NY - k, NY))] = early[k - 1] + late_in[k - 1].astype(F32)
    take(sent.at[7], early)
    take(sent.at[8], late_in)


def shards(captions, kv_weight, image_tokens, q_weight, context_grad, sample_prompt, caption_len):
    hbm = pl.BlockSpec(memory_space=pltpu.HBM)
    vmem = pl.BlockSpec(memory_space=pltpu.VMEM)
    dma = pltpu.SemaphoreType.DMA
    rows = SAMP * IMG

    context, image_grad, caption_grad = pl.pallas_call(
        kernel,
        out_shape=(
            pltpu.VMEM((rows, INNER), BF16),
            pltpu.VMEM((rows, CIMG), BF16),
            pltpu.VMEM((TOK, WIDE), F32),
        ),
        in_specs=[hbm] * 7,
        out_specs=(vmem,) * 3,
        scratch_shapes=[
            pltpu.SMEM(sample_prompt.shape, jnp.int32),
            pltpu.SMEM(caption_len.shape, jnp.int32),
            pltpu.VMEM((DEPTH, 2 * INNER), BF16),
            pltpu.VMEM((rows, CIMG), BF16),
            pltpu.VMEM((CIMG, INNER), BF16),
            pltpu.VMEM((rows, INNER), BF16),
            pltpu.VMEM((rows, INNER), BF16),
            pltpu.VMEM((rows, INNER), BF16),
            pltpu.VMEM((TOK, WIDE), BF16),
            pltpu.VMEM((NY, TOK, DEPTH), BF16),
            pltpu.VMEM((CHUNKS, NY, TOK, 2 * CW), F32),
            pltpu.VMEM((CHUNKS, NY - 1, TOK, 2 * CW), F32),
            pltpu.VMEM((CHUNKS, 2, TOK, CW), BF16),
            pltpu.VMEM((CHUNKS, NY * NC * SAMP, TOK, CW), BF16),
            pltpu.VMEM((CHUNKS, 2, SAMP, NY, TOK, CW), BF16),
            pltpu.VMEM((CHUNKS, 2, SAMP, NY, TOK, CW), BF16),
            pltpu.VMEM((CHUNKS, NY, NC, SAMP, TOK, CW), BF16),
            pltpu.VMEM((PROMPTS * TOK, NY * NC * SAMP * TOK), BF16),
            pltpu.VMEM((CHUNKS, NX, NZ, NC, TOK, CW), F32),
            pltpu.VMEM((CHUNKS, NX, NZ, NC, TOK, CW), BF16),
            pltpu.VMEM((CHUNKS, NX * NZ - 1, NC, TOK, CW), BF16),
            pltpu.VMEM((CHUNKS, NC, TOK, CW), BF16),
            pltpu.VMEM((CHUNKS, 2, NY, TOK, CW), BF16),
            pltpu.VMEM((NY, TOK, DEPTH), F32),
            pltpu.VMEM((NY, TOK, DEPTH), F32),
            pltpu.VMEM((NY, TOK, DEPTH), BF16),
            pltpu.VMEM((NY - 1, TOK, DEPTH), F32),
            pltpu.VMEM((NY - 1, TOK, DEPTH), BF16),
            dma((7,)),
            dma((9,)),
            dma,
            dma((CHUNKS,)),
            dma((CHUNKS,)),
            dma((CHUNKS,)),
            dma((CHUNKS,)),
            dma((CHUNKS,)),
            dma((CHUNKS,)),
            dma,
            dma,
            pltpu.SemaphoreType.REGULAR,
            pltpu.SemaphoreType.REGULAR,
        ] + [pltpu.VMEM((PROMPTS, TOK, CW), BF16) for _ in range(CHUNKS)],
        compiler_params=pltpu.CompilerParams(
            collective_id=0, has_side_effects=True, vmem_limit_bytes=VMEM_LIMIT
        ),
    )(*[
        pltpu.with_memory_space_constraint(operand, pltpu.HBM)
        for operand in (
            sample_prompt,
            caption_len,
            captions.reshape(TOK, WIDE),
            kv_weight,
            image_tokens.reshape(rows, CIMG),
            q_weight,
            context_grad.reshape(rows, INNER),
        )
    ])
    return (
        context.reshape(SAMP, IMG, INNER),
        image_grad.reshape(SAMP, IMG, CIMG),
        caption_grad.reshape(1, TOK, WIDE),
    )


def solution(mesh):
    placed = (
        P("dev", "grp", None),
        P("grp", None),
        P(("grp", "dev"), None, None),
        P(),
        P(("grp", "dev"), None, None),
        P(),
        P(),
    )
    return jax.shard_map(
        shards,
        mesh=mesh,
        in_specs=placed,
        out_specs=(
            P(("grp", "dev"), None, None),
            P(("grp", "dev"), None, None),
            P("dev", "grp", None),
        ),
        check_vma=False,
    )
```
